32 devices in a mesh: light: 2 (over y), view: 16 (over z, x, core).
Axes of the slice: x: 2, y: 2, z: 4, core: 2. Of those that a mesh axis runs over, the one named last changes fastest.
Arguments:
- density: bfloat16 [8, 256, 2048], P('light', 'view'), may hold values from 0 to 1
- occupied: int32 [2, 16, 16], P('light', 'view'), may hold values from 0 to 1, as said below
- view_sign: float32 [1], replicated, may hold values from -1 to 1, as said below
- transfer: float32 [4, 4], replicated, may hold values from -3 to 3
- absorb: float32 [3], replicated, may hold values from 0.5 to 20
- light_in: float32 [3, 256, 2048], P(None, 'view'), may hold values from 1 to 2.5
Outputs:
- image: float32 [4, 16384], P(None, ('light', 'view'))
The draws below stay inside these ranges and needn't reach their ends.
Inputs may be any that keep to these rules, and one draw needn't show every extreme that they name: `occupied`: 0 or 1; the share of occupied bricks differs from device to device. `view_sign`: magnitude 0.5 or more; either sign.
All inputs are finite; a program needn't handle non-finite values.
Results may differ from the reference program's by a relative error of at most 0.0003.
Values may be sent and summed in bfloat16 or wider, within the bound.
A program may use at most 64 MiB of HBM per device.

```python
import jax
import jax.numpy as jnp
from jax import lax

CX = 4
CY = 16
NZ = 2048
BRICK = 128
NX = 8
NY = 256
BRICKS = 16


def draw_occupied(key, part):
    level_key, ticket_key = jax.random.split(jax.random.fold_in(key, 7))
    level = jax.random.randint(level_key, (NX // CX, NY // CY, 1), 1, 5)
    ticket = jax.random.randint(ticket_key, (NX // CX, NY // CY, BRICKS), 0, 4)
    return (ticket < level).astype(jnp.int32)


def draw_view_sign(key, part):
    magnitude = jax.random.uniform(jax.random.fold_in(key, 11), (1,), jnp.float32, 0.5, 1.0)
    return magnitude


def draw_density(key, part):
    high_key, low_key, noise_key = jax.random.split(jax.random.fold_in(key, 13), 3)
    column = jnp.arange(NZ, dtype=jnp.int32)
    noise = jax.random.uniform(noise_key, (NX, NY, NZ), jnp.float32, 0.0, 1.0)
    pattern = column // 2 % 2
    high = jax.random.uniform(high_key, (NX, 1, NZ), jnp.float32, 0.82, 1.0)
    low = jax.random.uniform(low_key, (NX, 1, NZ), jnp.float32, 0.0, 0.1)
    base = jnp.where(pattern[None, None, :] == 1, high, low)
    value = 0.85 * base + 0.15 * noise
    return value.astype(jnp.bfloat16)


def draw_transfer(key, part):
    keys = jax.random.split(jax.random.fold_in(key, 17), 5)
    first = jax.random.uniform(keys[0], (1,), jnp.float32, -3.0, -2.5)
    second = jax.random.uniform(keys[1], (1,), jnp.float32, 2.5, 3.0)
    third = jax.random.uniform(keys[2], (1,), jnp.float32, 1.5, 3.0)
    fourth = jax.random.uniform(keys[3], (1,), jnp.float32, 1.5, 3.0)
    extinction_row = jnp.concatenate([first, second, third, fourth])[None, :]
    colour_rows = jax.random.truncated_normal(keys[4], -3.0, 3.0, (3, 4), jnp.float32)
    return jnp.concatenate([extinction_row, colour_rows], axis=0)


def draw_absorb(key, part):
    keys = jax.random.split(jax.random.fold_in(key, 19), 4)
    bounds = ((0.5, 1.5), (3.0, 8.0), (12.0, 20.0))
    values = []
    for index in range(3):
        lower, upper = bounds[index]
        exponent = jax.random.uniform(keys[index], (1,), jnp.float32, jnp.log(lower), jnp.log(upper))
        values.append(jnp.clip(jnp.exp(exponent), lower, upper))
    stacked = jnp.concatenate(values)
    order = jax.random.permutation(keys[3], 3)
    return stacked[order]


def block_scale(stream_key, extent, cuts, least, top_value):
    factor_of, own = 1.0, jax.random.fold_in(stream_key, 6)
    for axis_at, shards_of in cuts:
        heights = jnp.exp(jax.random.uniform(jax.random.fold_in(own, axis_at), (shards_of,), jnp.float32, least / len(cuts), top_value / len(cuts)))
        factor_of = factor_of * jnp.repeat(heights, extent[axis_at] // shards_of).reshape([-1 if axis == axis_at else 1 for axis in range(len(extent))])
    return factor_of


def setup_inputs(seed: int = 0) -> dict:
    seeds = jax.random.split(jax.random.key(seed), 7)
    density = draw_density(jax.random.fold_in(seeds[6], 71), 0)
    occupied = draw_occupied(jax.random.fold_in(seeds[6], 71), 0)
    view_sign = draw_view_sign(jax.random.fold_in(seeds[6], 71), 0)
    transfer = draw_transfer(jax.random.fold_in(seeds[6], 71), 0)
    absorb = draw_absorb(jax.random.fold_in(seeds[6], 71), 0)
    light_in = jnp.clip(1.0 + 1.5 * jax.random.uniform(seeds[5], (3, NY, NZ), jnp.float32) ** block_scale(seeds[5], (3, NY, NZ), ((1, 16),), -0.2, 0.2), 1.0, 2.5)
    return {"density": density, "occupied": occupied, "view_sign": view_sign, "transfer": transfer, "absorb": absorb, "light_in": light_in}


def polynomial(coeffs, values):
    return coeffs[0] + values * (coeffs[1] + values * (coeffs[2] + values * coeffs[3]))

def blur_columns(field):
    widths = [(0, 0)] * (field.ndim - 1) + [(1, 1)]
    padded = jnp.pad(field, widths)
    return 0.25 * padded[..., :-2] + 0.5 * padded[..., 1:-1] + 0.25 * padded[..., 2:]

def composite_depth(emitted, opacity, facing_back):
    emitted = jnp.where(facing_back == 1, jnp.flip(emitted, 1), emitted)
    opacity = jnp.where(facing_back == 1, jnp.flip(opacity, 0), opacity)
    passing = 1.0 - opacity
    through = jnp.cumprod(passing, axis=0)
    before = jnp.concatenate([jnp.ones_like(passing[:1]), through[:-1]], axis=0)
    colour = lax.optimization_barrier(jnp.sum(before[None] * emitted, axis=1))
    return jnp.concatenate([colour, (1.0 - through[-1])[None]], axis=0)

def reference(density, occupied, view_sign, transfer, absorb, light_in):
    padded = jnp.pad(density, ((1, 1), (0, 0), (0, 0)))
    occupancy_all = jnp.repeat(occupied.astype(jnp.float32), BRICK, axis=2)
    occupancy_all = jnp.repeat(occupancy_all, CY, axis=1)
    facing_back = (view_sign[0] < 0.0).astype(jnp.int32)
    path_length = 2.0 / NY / jnp.abs(view_sign[0])

    def layer(light_front, layer_row):
        window = lax.dynamic_slice_in_dim(padded, layer_row, 3, 0).astype(jnp.float32)
        centre = window[1]
        occupancy = lax.dynamic_index_in_dim(occupancy_all, layer_row // CX, 0, keepdims=False)
        grad_x = 0.5 * (window[2] - window[0])
        bricked = centre.reshape(NY // CY, CY, NZ)
        side_y = jnp.pad(bricked, ((0, 0), (1, 1), (0, 0)), mode='edge')
        grad_y = (0.5 * (side_y[:, 2:, :] - side_y[:, :-2, :])).reshape(NY, NZ)
        side_z = jnp.pad(centre, ((0, 0), (1, 1)))
        grad_z = 0.5 * (side_z[:, 2:] - side_z[:, :-2])
        extinction = jax.nn.softplus(polynomial(transfer[0], centre)) * occupancy
        opacity = 1.0 - jnp.exp(-extinction * path_length)
        colour = jnp.stack([jax.nn.sigmoid(polynomial(transfer[channel], centre)) for channel in (1, 2, 3)], axis=0)
        facing = (0.8 * grad_x + 0.36 * grad_y + 0.48 * grad_z) * lax.rsqrt(1.0 + grad_x * grad_x + grad_y * grad_y + grad_z * grad_z)
        shading = 0.65 + 0.35 * facing
        transmit = jnp.exp(-absorb[:, None, None] * extinction[None] / NX)
        emitted = opacity[None] * colour * (0.2 + light_front * shading[None])
        pixel_row = composite_depth(emitted, opacity, facing_back)
        return (blur_columns(light_front * transmit), pixel_row)
    _, pixel_rows = lax.scan(layer, light_in, jnp.arange(NX, dtype=jnp.int32))
    return jnp.transpose(pixel_rows, (1, 0, 2)).reshape(4, NX * NZ)
```

```python
import functools

import jax
import jax.numpy as jnp
from jax import lax
from jax.experimental import pallas as pl
from jax.experimental.pallas import tpu as pltpu
from jax.sharding import PartitionSpec as P

LANES = 128
HALF = LANES // 2
LOG2E = 1.4426950408889634
MESH = pl.DeviceIdType.MESH


class Plan:
    def __init__(self, lights, views, cells_x, cells_y, columns, bricks):
        self.lights, self.views = lights, views
        self.cx, self.cy = cells_x, cells_y
        self.nx, self.ny = cells_x * lights, cells_y * views
        self.tiles = columns // LANES
        self.rows = self.tiles // lights
        self.win_tiles = self.rows + (2 if lights > 2 else 1)
        self.width = self.win_tiles * LANES
        self.piece_rows = cells_x * self.tiles // views
        self.groups = self.rows // self.piece_rows
        self.per_layer = self.tiles // self.piece_rows
        self.tiles_per_brick = self.tiles // bricks
        self.bricks = bricks

    def window(self, light):
        return jnp.clip(light * self.rows - 1, 0, self.tiles - self.win_tiles)


def cubic(coeffs, x):
    return coeffs[0] + x * (coeffs[1] + x * (coeffs[2] + x * coeffs[3]))


def recip(x):
    r = pltpu.reciprocal(x, approx=True)
    return r * (2.0 - x * r)


def kernel(
    plan,
    density,
    occupied,
    view_sign,
    transfer,
    absorb,
    light_in,
    out,
    wbuf,
    lbuf,
    occ,
    dens,
    slope_z,
    front,
    edge_front,
    edge_prod,
    image,
    recv,
    dsem,
    dsend,
    osem,
    osend,
    lsem,
    isend,
    rsem,
):
    lights, views, rows, cy = plan.lights, plan.views, plan.rows, plan.cy
    me_l = lax.axis_index("light")
    me_v = lax.axis_index("view")
    win = plan.window(me_l)
    off = me_l * rows - win
    slab_of_me = ((me_v * plan.piece_rows) % plan.tiles) // rows

    barrier = pltpu.get_barrier_semaphore()
    for k in range(1, lights):
        pl.semaphore_signal(
            barrier, inc=1, device_id={"light": (me_l + k) % lights, "view": me_v}, device_id_type=MESH
        )

    def greet(v, carry):
        @pl.when(jnp.logical_or(v != me_v, slab_of_me != me_l))
        def _():
            pl.semaphore_signal(
                barrier, inc=1, device_id={"light": slab_of_me, "view": v}, device_id_type=MESH
            )

        return carry

    lax.fori_loop(0, views, greet, 0)

    def columns_of(light):
        return pl.ds(pl.multiple_of(plan.window(light) * LANES, LANES), plan.width)

    for i in range(plan.cx):
        layer = me_l * plan.cx + i
        pltpu.make_async_copy(
            density.at[i, :, columns_of(me_l)], wbuf.at[layer], dsem.at[layer]
        ).start()
    light_copy = pltpu.make_async_copy(light_in.at[:, :, columns_of(me_l)], lbuf, lsem)
    light_copy.start()

    for k in range(plan.bricks):
        value = jnp.full((plan.tiles_per_brick, LANES), occupied[0, 0, k].astype(jnp.float32))
        occ[me_l, k * plan.tiles_per_brick : (k + 1) * plan.tiles_per_brick, :] = value

    @pl.when(slab_of_me == me_l)
    def _():
        pl.semaphore_wait(barrier, lights - 1 + views - 1)

    @pl.when(slab_of_me != me_l)
    def _():
        pl.semaphore_wait(barrier, lights - 1 + views)

    def occ_copy(k):
        return pltpu.make_async_remote_copy(
            src_ref=occ.at[me_l],
            dst_ref=occ.at[me_l],
            send_sem=osend.at[k],
            recv_sem=osem.at[me_l],
            device_id={"light": (me_l + k) % lights, "view": me_v},
            device_id_type=MESH,
        )

    def dens_copy(k, i):
        other = (me_l + k) % lights
        layer = me_l * plan.cx + i
        return pltpu.make_async_remote_copy(
            src_ref=density.at[i, :, columns_of(other)],
            dst_ref=wbuf.at[layer],
            send_sem=dsend.at[k, i],
            recv_sem=dsem.at[layer],
            device_id={"light": other, "view": me_v},
            device_id_type=MESH,
        )

    for k in range(1, lights):
        occ_copy(k).start()
    for i in range(plan.cx):
        for k in range(1, lights):
            dens_copy(k, i).start()

    core = (rows, LANES)
    lane = lax.broadcasted_iota(jnp.int32, core, 1)
    sub = lax.broadcasted_iota(jnp.int32, core, 0)
    first_lane, last_lane = lane == 0, lane == LANES - 1
    first_row, last_row = sub == 0, sub == rows - 1
    flat = (cy, LANES)
    flat_lane = lax.broadcasted_iota(jnp.int32, flat, 1)
    flat_first, flat_last = flat_lane == 0, flat_lane == LANES - 1
    flat_low = flat_lane < HALF
    sign = jnp.full(core, view_sign[0])
    facing_back = sign < 0.0
    path_rate = (-2.0 * LOG2E / plan.ny) / jnp.abs(sign)
    rates = [absorb[c] * (-LOG2E / plan.nx) for c in range(3)]
    ext_coeffs = [transfer[0, k] * LOG2E for k in range(4)]
    colour_coeffs = [[transfer[c, k] * (-LOG2E) for k in range(4)] for c in (1, 2, 3)]
    has_left = jnp.where(me_l > 0, 1.0, 0.0)
    has_right = jnp.where(me_l < lights - 1, 1.0, 0.0)
    edge_tiles = [jnp.maximum(off - 1, 0)]
    if lights > 2:
        edge_tiles = [jnp.maximum(off - 1, 0), jnp.minimum(off + rows - 1, plan.win_tiles - 2)]
    else:
        edge_tiles = [jnp.where(me_l == 0, rows - 1, 0)]

    zeros = jnp.zeros((cy * rows, LANES), jnp.float32)
    dens[0] = zeros
    dens[plan.nx + 1] = zeros

    def tile_at(ref, lead, t):
        return ref[lead, :, pl.ds(pl.multiple_of(t * LANES, LANES), LANES)].astype(jnp.float32)

    def straddle(a, b):
        return pltpu.roll(jnp.where(flat_low, b, a), HALF, 1)

    def wait_layer(x):
        pltpu.make_async_copy(wbuf.at[x], wbuf.at[x], dsem.at[x]).wait()

    def spread(x):
        tiles = [tile_at(wbuf, x, jnp.maximum(off - 1, 0)) * has_left]
        tiles += [tile_at(wbuf, x, off + t) for t in range(rows)]
        tiles += [tile_at(wbuf, x, jnp.minimum(off + rows, plan.win_tiles - 1)) * has_right]
        for t in range(rows):
            here = tiles[t + 1]
            after = pltpu.roll(jnp.where(flat_first, tiles[t + 2], here), LANES - 1, 1)
            before = pltpu.roll(jnp.where(flat_last, tiles[t], here), 1, 1)
            dens[x + 1, pl.ds(t, cy, stride=rows), :] = here
            slope_z[x % 2, pl.ds(t, cy, stride=rows), :] = after - before

    def wait_occ(block):
        @pl.when(block != me_l)
        def _():
            pltpu.make_async_copy(occ.at[block], occ.at[block], osem.at[block]).wait()

    light_copy.wait()
    for c in range(3):
        for t in range(rows):
            front[c, pl.ds(t, cy, stride=rows), :] = tile_at(lbuf, c, off + t)
        for e, t in enumerate(edge_tiles):
            edge_front[e, c] = straddle(tile_at(lbuf, c, t), tile_at(lbuf, c, t + 1))

    wait_layer(0)
    spread(0)

    def do_layer(x, carry):
        block = x // plan.cx

        @pl.when(x % plan.cx == 0)
        def _():
            wait_occ(block)

        @pl.when(x + 1 < plan.nx)
        def _():
            wait_layer(x + 1)
            spread(x + 1)

        for e, t in enumerate(edge_tiles):
            cells = straddle(tile_at(wbuf, x, t), tile_at(wbuf, x, t + 1))
            held_a = occ[block, pl.ds(win + t, 1), :]
            held_b = occ[block, pl.ds(win + t + 1, 1), :]
            held = jnp.where(flat_low[:1], held_a, held_b)
            ext = jnp.log(1.0 + jnp.exp2(cubic(ext_coeffs, cells))) * held
            for c in range(3):
                prod = edge_front[e, c] * jnp.exp2(rates[c] * ext)
                seam = pltpu.roll(prod, HALF, 1)
                if e == 0:
                    edge_prod[0, c] = seam * has_left
                if e == len(edge_tiles) - 1:
                    edge_prod[1, c] = seam * has_right
                edge_front[e, c] = 0.5 * prod + 0.25 * (
                    pltpu.roll(prod, 1, 1) + pltpu.roll(prod, LANES - 1, 1)
                )

        held = occ[block, pl.ds(pl.multiple_of(me_l * rows, rows), rows), :]
        through = jnp.ones(core, jnp.float32)
        acc = [jnp.zeros(core, jnp.float32) for _ in range(3)]

        def at(layer, y):
            return dens[layer, y * rows : (y + 1) * rows, :]

        for y in range(cy):
            d = at(x + 1, y)
            gx = at(x + 2, y) - at(x, y)
            gy = at(x + 1, min(y + 1, cy - 1)) - at(x + 1, max(y - 1, 0))
            gz = slope_z[x % 2, y * rows : (y + 1) * rows, :]
            facing = (0.28 * gx + 0.126 * gy + 0.168 * gz) * lax.rsqrt(
                4.0 + gx * gx + gy * gy + gz * gz
            )
            shading = 0.65 + facing
            ext = jnp.log(1.0 + jnp.exp2(cubic(ext_coeffs, d))) * held
            passing = jnp.exp2(path_rate * ext)
            weight = jnp.where(facing_back, 1.0, through) * (1.0 - passing)
            keep = jnp.where(facing_back, passing, 1.0)
            through = through * passing
            for c in range(3):
                colour = recip(1.0 + jnp.exp2(cubic(colour_coeffs[c], d)))
                f = front[c, y * rows : (y + 1) * rows, :]
                acc[c] = keep * acc[c] + (weight * colour) * (0.2 + f * shading)
                prod = f * jnp.exp2(rates[c] * ext)
                seam_l = edge_prod[0, c, y : y + 1, :]
                seam_r = edge_prod[1, c, y : y + 1, :]
                up = jnp.where(first_row, seam_l, pltpu.roll(prod, 1, 0))
                down = jnp.where(last_row, seam_r, pltpu.roll(prod, rows - 1, 0))
                before = pltpu.roll(jnp.where(last_lane, up, prod), 1, 1)
                after = pltpu.roll(jnp.where(first_lane, down, prod), LANES - 1, 1)
                front[c, y * rows : (y + 1) * rows, :] = 0.5 * prod + 0.25 * (before + after)

        pixels = acc + [1.0 - through]
        n = plan.piece_rows
        for j in range(plan.groups):
            for c in range(4):
                image[x, j, c * n : (c + 1) * n, :] = pixels[c][j * n : (j + 1) * n, :]
        for j in range(plan.groups):
            send_piece(x, j, True)
        return carry

    def send_piece(x, j, start):
        owner_l = x // plan.cx
        owner_v = (x % plan.cx) * plan.per_layer + me_l * plan.groups + j
        mine = jnp.logical_and(owner_l == me_l, owner_v == me_v)

        @pl.when(mine)
        def _():
            if start:
                pltpu.make_async_copy(image.at[x, j], recv.at[me_v], rsem.at[me_v]).start()

        @pl.when(jnp.logical_not(mine))
        def _():
            copy = pltpu.make_async_remote_copy(
                src_ref=image.at[x, j],
                dst_ref=recv.at[me_v],
                send_sem=isend.at[x, j],
                recv_sem=rsem.at[me_v],
                device_id={"light": owner_l, "view": owner_v},
                device_id_type=MESH,
            )
            if start:
                copy.start()
            else:
                copy.wait_send()

    lax.fori_loop(0, plan.nx, do_layer, 0)

    n = plan.piece_rows
    small = (n, LANES)
    back = jnp.full(small, view_sign[0]) < 0.0

    def merge(v, carry):
        pltpu.make_async_copy(recv.at[v], recv.at[v], rsem.at[v]).wait()
        through, acc = carry[0], carry[1:]
        passing = 1.0 - recv[v, 3 * n : 4 * n, :]
        weight = jnp.where(back, 1.0, through)
        keep = jnp.where(back, passing, 1.0)
        acc = [keep * acc[c] + weight * recv[v, c * n : (c + 1) * n, :] for c in range(3)]
        return (through * passing, *acc)

    zero = jnp.zeros(small, jnp.float32)
    merged = lax.fori_loop(0, views, merge, (jnp.ones(small, jnp.float32), zero, zero, zero))
    pixels = list(merged[1:]) + [1.0 - merged[0]]
    for c in range(4):
        for r in range(n):
            out[c : c + 1, r * LANES : (r + 1) * LANES] = pixels[c][r : r + 1, :]

    def finish(x, carry):
        for j in range(plan.groups):
            send_piece(x, j, False)
        return carry

    lax.fori_loop(0, plan.nx, finish, 0)
    for k in range(1, lights):
        occ_copy(k).wait_send()
        for i in range(plan.cx):
            dens_copy(k, i).wait_send()


def body(density, occupied, view_sign, transfer, absorb, light_in):
    cells_x, cells_y, columns = density.shape
    plan = Plan(
        lax.axis_size("light"), lax.axis_size("view"), cells_x, cells_y, columns, occupied.shape[2]
    )
    lights, views = plan.lights, plan.views
    n = plan.piece_rows
    edges = 2 if lights > 2 else 1
    f32 = jnp.float32
    smem = pl.BlockSpec(memory_space=pltpu.SMEM)
    hbm = pl.BlockSpec(memory_space=pl.ANY)
    dma = pltpu.SemaphoreType.DMA
    return pl.pallas_call(
        functools.partial(kernel, plan),
        out_shape=jax.ShapeDtypeStruct((4, n * LANES), f32),
        in_specs=[hbm, smem, smem, smem, smem, hbm],
        out_specs=pl.BlockSpec(memory_space=pltpu.VMEM),
        scratch_shapes=[
            pltpu.VMEM((plan.nx, cells_y, plan.width), density.dtype),
            pltpu.VMEM((3, cells_y, plan.width), f32),
            pltpu.VMEM((lights, plan.tiles, LANES), f32),
            pltpu.VMEM((plan.nx + 2, cells_y * plan.rows, LANES), f32),
            pltpu.VMEM((2, cells_y * plan.rows, LANES), f32),
            pltpu.VMEM((3, cells_y * plan.rows, LANES), f32),
            pltpu.VMEM((edges, 3, cells_y, LANES), f32),
            pltpu.VMEM((2, 3, cells_y, LANES), f32),
            pltpu.VMEM((plan.nx, plan.groups, 4 * n, LANES), f32),
            pltpu.VMEM((views, 4 * n, LANES), f32),
            dma((plan.nx,)),
            dma((lights, cells_x)),
            dma((lights,)),
            dma((lights,)),
            dma(()),
            dma((plan.nx, plan.groups)),
            dma((views,)),
        ],
        compiler_params=pltpu.CompilerParams(
            collective_id=0, has_side_effects=True, vmem_limit_bytes=32 * 1024 * 1024
        ),
    )(density, occupied, view_sign, transfer, absorb, light_in)


def solution(mesh):
    in_specs = (
        P("light", "view", None),
        P("light", "view", None),
        P(),
        P(),
        P(),
        P(None, "view", None),
    )
    out_specs = P(None, ("light", "view"))
    return jax.shard_map(body, mesh=mesh, in_specs=in_specs, out_specs=out_specs, check_vma=False)
```

```python
import functools

import jax
import jax.numpy as jnp
from jax import lax
from jax.experimental import pallas as pl
from jax.experimental.pallas import tpu as pltpu
from jax.sharding import PartitionSpec as P

LANES = 128
HALF = LANES // 2
LOG2E = 1.4426950408889634
MESH = pl.DeviceIdType.MESH


class Plan:
    def __init__(self, lights, views, cells_x, cells_y, columns, bricks):
        self.lights, self.views = lights, views
        self.cx, self.cy = cells_x, cells_y
        self.nx, self.ny = cells_x * lights, cells_y * views
        self.tiles = columns // LANES
        self.rows = self.tiles // lights
        self.win_tiles = self.rows + (2 if lights > 2 else 1)
        self.width = self.win_tiles * LANES
        self.piece_rows = cells_x * self.tiles // views
        self.groups = self.rows // self.piece_rows
        self.per_layer = self.tiles // self.piece_rows
        self.tiles_per_brick = self.tiles // bricks
        self.bricks = bricks

    def window(self, light):
        return jnp.clip(light * self.rows - 1, 0, self.tiles - self.win_tiles)


def cubic(coeffs, x):
    return coeffs[0] + x * (coeffs[1] + x * (coeffs[2] + x * coeffs[3]))


def recip(x):
    r = pltpu.reciprocal(x, approx=True)
    return r * (2.0 - x * r)


def kernel(
    plan,
    density,
    occupied_hbm,
    view_sign_hbm,
    transfer_hbm,
    absorb_hbm,
    light_in,
    out,
    occupied,
    view_sign,
    transfer,
    absorb,
    wbuf,
    lbuf,
    occ,
    dens,
    slope_z,
    front,
    edge_front,
    edge_prod,
    image,
    recv,
    dsem,
    dsend,
    osem,
    osend,
    lsem,
    isend,
    rsem,
):
    lights, views, rows, cy = plan.lights, plan.views, plan.rows, plan.cy
    me_l = lax.axis_index("light")
    me_v = lax.axis_index("view")
    win = plan.window(me_l)
    off = me_l * rows - win
    slab_of_me = ((me_v * plan.piece_rows) % plan.tiles) // rows

    small_copies = [
        pltpu.make_async_copy(src, dst, lsem.at[i])
        for i, (src, dst) in enumerate(
            (
                (occupied_hbm, occupied),
                (view_sign_hbm, view_sign),
                (transfer_hbm, transfer),
                (absorb_hbm, absorb),
            )
        )
    ]
    for copy in small_copies:
        copy.start()

    barrier = pltpu.get_barrier_semaphore()
    for k in range(1, lights):
        pl.semaphore_signal(
            barrier, inc=1, device_id={"light": (me_l + k) % lights, "view": me_v}, device_id_type=MESH
        )

    def greet(v, carry):
        @pl.when(jnp.logical_or(v != me_v, slab_of_me != me_l))
        def _():
            pl.semaphore_signal(
                barrier, inc=1, device_id={"light": slab_of_me, "view": v}, device_id_type=MESH
            )

        return carry

    lax.fori_loop(0, views, greet, 0)

    def columns_of(light):
        return pl.ds(pl.multiple_of(plan.window(light) * LANES, LANES), plan.width)

    for i in range(plan.cx):
        layer = me_l * plan.cx + i
        pltpu.make_async_copy(
            density.at[i, :, columns_of(me_l)], wbuf.at[layer], dsem.at[layer]
        ).start()
    light_copy = pltpu.make_async_copy(light_in.at[:, :, columns_of(me_l)], lbuf, lsem.at[4])
    light_copy.start()

    for copy in small_copies:
        copy.wait()
    for k in range(plan.bricks):
        value = jnp.full((plan.tiles_per_brick, LANES), occupied[0, 0, k].astype(jnp.float32))
        occ[me_l, k * plan.tiles_per_brick : (k + 1) * plan.tiles_per_brick, :] = value

    @pl.when(slab_of_me == me_l)
    def _():
        pl.semaphore_wait(barrier, lights - 1 + views - 1)

    @pl.when(slab_of_me != me_l)
    def _():
        pl.semaphore_wait(barrier, lights - 1 + views)

    def occ_copy(k):
        return pltpu.make_async_remote_copy(
            src_ref=occ.at[me_l],
            dst_ref=occ.at[me_l],
            send_sem=osend.at[k],
            recv_sem=osem.at[me_l],
            device_id={"light": (me_l + k) % lights, "view": me_v},
            device_id_type=MESH,
        )

    def dens_copy(k, i):
        other = (me_l + k) % lights
        layer = me_l * plan.cx + i
        return pltpu.make_async_remote_copy(
            src_ref=density.at[i, :, columns_of(other)],
            dst_ref=wbuf.at[layer],
            send_sem=dsend.at[k, i],
            recv_sem=dsem.at[layer],
            device_id={"light": other, "view": me_v},
            device_id_type=MESH,
        )

    for k in range(1, lights):
        occ_copy(k).start()
    for i in range(plan.cx):
        for k in range(1, lights):
            dens_copy(k, i).start()

    core = (rows, LANES)
    lane = lax.broadcasted_iota(jnp.int32, core, 1)
    sub = lax.broadcasted_iota(jnp.int32, core, 0)
    first_lane, last_lane = lane == 0, lane == LANES - 1
    first_row, last_row = sub == 0, sub == rows - 1
    flat = (cy, LANES)
    flat_lane = lax.broadcasted_iota(jnp.int32, flat, 1)
    flat_first, flat_last = flat_lane == 0, flat_lane == LANES - 1
    flat_low = flat_lane < HALF
    sign = jnp.full(core, view_sign[0])
    facing_back = sign < 0.0
    path_rate = (-2.0 * LOG2E / plan.ny) / jnp.abs(sign)
    rates = [absorb[c] * (-LOG2E / plan.nx) for c in range(3)]
    ext_coeffs = [transfer[0, k] * LOG2E for k in range(4)]
    colour_coeffs = [[transfer[c, k] * (-LOG2E) for k in range(4)] for c in (1, 2, 3)]
    has_left = jnp.where(me_l > 0, 1.0, 0.0)
    has_right = jnp.where(me_l < lights - 1, 1.0, 0.0)
    edge_tiles = [jnp.maximum(off - 1, 0)]
    if lights > 2:
        edge_tiles = [jnp.maximum(off - 1, 0), jnp.minimum(off + rows - 1, plan.win_tiles - 2)]
    else:
        edge_tiles = [jnp.where(me_l == 0, rows - 1, 0)]

    zeros = jnp.zeros((cy * rows, LANES), jnp.float32)
    dens[0] = zeros

    def tile_at(ref, lead, t):
        return ref[lead, :, pl.ds(pl.multiple_of(t * LANES, LANES), LANES)].astype(jnp.float32)

    def straddle(a, b):
        return pltpu.roll(jnp.where(flat_low, b, a), HALF, 1)

    def wait_layer(x):
        pltpu.make_async_copy(wbuf.at[x], wbuf.at[x], dsem.at[x]).wait()

    def spread(x):
        inside = jnp.where(x < plan.nx, 1.0, 0.0)
        layer = jnp.minimum(x, plan.nx - 1)
        tiles = [tile_at(wbuf, layer, jnp.maximum(off - 1, 0)) * has_left]
        tiles += [tile_at(wbuf, layer, off + t) for t in range(rows)]
        tiles += [tile_at(wbuf, layer, jnp.minimum(off + rows, plan.win_tiles - 1)) * has_right]
        for t in range(rows):
            here = tiles[t + 1]
            after = pltpu.roll(jnp.where(flat_first, tiles[t + 2], here), LANES - 1, 1)
            before = pltpu.roll(jnp.where(flat_last, tiles[t], here), 1, 1)
            dens[x + 1, pl.ds(t, cy, stride=rows), :] = here * inside
            slope_z[x % 2, pl.ds(t, cy, stride=rows), :] = after - before

    def wait_occ(block):
        @pl.when(block != me_l)
        def _():
            pltpu.make_async_copy(occ.at[block], occ.at[block], osem.at[block]).wait()

    def cross(x):
        layer = jnp.minimum(x, plan.nx - 1)
        block = layer // plan.cx
        for e, t in enumerate(edge_tiles):
            cells = straddle(tile_at(wbuf, layer, t), tile_at(wbuf, layer, t + 1))
            held_a = occ[block, pl.ds(win + t, 1), :]
            held_b = occ[block, pl.ds(win + t + 1, 1), :]
            held = jnp.where(flat_low[:1], held_a, held_b)
            ext = jnp.log(1.0 + jnp.exp2(cubic(ext_coeffs, cells))) * held
            for c in range(3):
                prod = edge_front[e, c] * jnp.exp2(rates[c] * ext)
                seam = pltpu.roll(prod, HALF, 1)
                if e == 0:
                    edge_prod[x % 2, 0, c] = seam * has_left
                if e == len(edge_tiles) - 1:
                    edge_prod[x % 2, 1, c] = seam * has_right
                edge_front[e, c] = 0.5 * prod + 0.25 * (
                    pltpu.roll(prod, 1, 1) + pltpu.roll(prod, LANES - 1, 1)
                )

    light_copy.wait()
    for c in range(3):
        for t in range(rows):
            front[c, pl.ds(t, cy, stride=rows), :] = tile_at(lbuf, c, off + t)
        for e, t in enumerate(edge_tiles):
            edge_front[e, c] = straddle(tile_at(lbuf, c, t), tile_at(lbuf, c, t + 1))

    wait_layer(0)
    wait_occ(0)
    spread(0)
    cross(0)

    def do_layer(x, carry):
        block = x // plan.cx

        @pl.when(x + 1 < plan.nx)
        def _():
            wait_layer(x + 1)

        @pl.when(jnp.logical_and(x + 1 < plan.nx, (x + 1) % plan.cx == 0))
        def _():
            wait_occ((x + 1) // plan.cx)

        spread(x + 1)
        cross(x + 1)

        held = occ[block, pl.ds(pl.multiple_of(me_l * rows, rows), rows), :]
        acc = [jnp.zeros(core, jnp.float32) for _ in range(3)]

        def at(layer, y):
            return dens[layer, y * rows : (y + 1) * rows, :]

        exts = [
            jnp.log(1.0 + jnp.exp2(cubic(ext_coeffs, at(x + 1, y)))) * held for y in range(cy)
        ]
        passing = [jnp.exp2(path_rate * ext) for ext in exts]
        in_front = [jnp.ones(core, jnp.float32)]
        behind = [jnp.ones(core, jnp.float32)]
        for y in range(cy):
            in_front.append(in_front[-1] * passing[y])
            behind.append(behind[-1] * passing[cy - 1 - y])
        weights = [
            jnp.where(facing_back, behind[cy - 1 - y], in_front[y]) * (1.0 - passing[y])
            for y in range(cy)
        ]
        through = in_front[cy]

        for y in range(cy):
            d = at(x + 1, y)
            gx = at(x + 2, y) - at(x, y)
            gy = at(x + 1, min(y + 1, cy - 1)) - at(x + 1, max(y - 1, 0))
            gz = slope_z[x % 2, y * rows : (y + 1) * rows, :]
            facing = (0.28 * gx + 0.126 * gy + 0.168 * gz) * lax.rsqrt(
                4.0 + gx * gx + gy * gy + gz * gz
            )
            shading = 0.65 + facing
            for c in range(3):
                colour = recip(1.0 + jnp.exp2(cubic(colour_coeffs[c], d)))
                f = front[c, y * rows : (y + 1) * rows, :]
                acc[c] = acc[c] + (weights[y] * colour) * (0.2 + f * shading)
                prod = f * jnp.exp2(rates[c] * exts[y])
                seam_l = edge_prod[x % 2, 0, c, y : y + 1, :]
                seam_r = edge_prod[x % 2, 1, c, y : y + 1, :]
                up = jnp.where(first_row, seam_l, pltpu.roll(prod, 1, 0))
                down = jnp.where(last_row, seam_r, pltpu.roll(prod, rows - 1, 0))
                before = pltpu.roll(jnp.where(last_lane, up, prod), 1, 1)
                after = pltpu.roll(jnp.where(first_lane, down, prod), LANES - 1, 1)
                front[c, y * rows : (y + 1) * rows, :] = 0.5 * prod + 0.25 * (before + after)

        pixels = acc + [1.0 - through]
        n = plan.piece_rows
        for j in range(plan.groups):
            for c in range(4):
                image[x, j, c * n : (c + 1) * n, :] = pixels[c][j * n : (j + 1) * n, :]
        for j in range(plan.groups):
            send_piece(x, j, True)
        return carry

    def send_piece(x, j, start):
        owner_l = x // plan.cx
        owner_v = (x % plan.cx) * plan.per_layer + me_l * plan.groups + j
        mine = jnp.logical_and(owner_l == me_l, owner_v == me_v)

        @pl.when(mine)
        def _():
            if start:
                pltpu.make_async_copy(image.at[x, j], recv.at[me_v], rsem.at[me_v]).start()

        @pl.when(jnp.logical_not(mine))
        def _():
            copy = pltpu.make_async_remote_copy(
                src_ref=image.at[x, j],
                dst_ref=recv.at[me_v],
                send_sem=isend.at[x, j],
                recv_sem=rsem.at[me_v],
                device_id={"light": owner_l, "view": owner_v},
                device_id_type=MESH,
            )
            if start:
                copy.start()
            else:
                copy.wait_send()

    lax.fori_loop(0, plan.nx, do_layer, 0)

    n = plan.piece_rows
    small = (n, LANES)
    back = jnp.full(small, view_sign[0]) < 0.0

    def merge(v, carry):
        pltpu.make_async_copy(recv.at[v], recv.at[v], rsem.at[v]).wait()
        through, acc = carry[0], carry[1:]
        passing = 1.0 - recv[v, 3 * n : 4 * n, :]
        weight = jnp.where(back, 1.0, through)
        keep = jnp.where(back, passing, 1.0)
        acc = [keep * acc[c] + weight * recv[v, c * n : (c + 1) * n, :] for c in range(3)]
        return (through * passing, *acc)

    zero = jnp.zeros(small, jnp.float32)
    merged = lax.fori_loop(0, views, merge, (jnp.ones(small, jnp.float32), zero, zero, zero))
    pixels = list(merged[1:]) + [1.0 - merged[0]]
    for c in range(4):
        for r in range(n):
            out[c : c + 1, r * LANES : (r + 1) * LANES] = pixels[c][r : r + 1, :]

    def finish(x, carry):
        for j in range(plan.groups):
            send_piece(x, j, False)
        return carry

    lax.fori_loop(0, plan.nx, finish, 0)
    for k in range(1, lights):
        occ_copy(k).wait_send()
        for i in range(plan.cx):
            dens_copy(k, i).wait_send()


def body(density, occupied, view_sign, transfer, absorb, light_in):
    cells_x, cells_y, columns = density.shape
    plan = Plan(
        lax.axis_size("light"), lax.axis_size("view"), cells_x, cells_y, columns, occupied.shape[2]
    )
    lights, views = plan.lights, plan.views
    n = plan.piece_rows
    edges = 2 if lights > 2 else 1
    f32 = jnp.float32
    hbm = pl.BlockSpec(memory_space=pl.ANY)
    dma = pltpu.SemaphoreType.DMA
    return pl.pallas_call(
        functools.partial(kernel, plan),
        out_shape=jax.ShapeDtypeStruct((4, n * LANES), f32),
        in_specs=[hbm] * 6,
        out_specs=pl.BlockSpec(memory_space=pltpu.VMEM),
        scratch_shapes=[
            pltpu.SMEM(occupied.shape, occupied.dtype),
            pltpu.SMEM(view_sign.shape, f32),
            pltpu.SMEM(transfer.shape, f32),
            pltpu.SMEM(absorb.shape, f32),
            pltpu.VMEM((plan.nx, cells_y, plan.width), density.dtype),
            pltpu.VMEM((3, cells_y, plan.width), f32),
            pltpu.VMEM((lights, plan.tiles, LANES), f32),
            pltpu.VMEM((plan.nx + 2, cells_y * plan.rows, LANES), f32),
            pltpu.VMEM((2, cells_y * plan.rows, LANES), f32),
            pltpu.VMEM((3, cells_y * plan.rows, LANES), f32),
            pltpu.VMEM((edges, 3, cells_y, LANES), f32),
            pltpu.VMEM((2, 2, 3, cells_y, LANES), f32),
            pltpu.VMEM((plan.nx, plan.groups, 4 * n, LANES), f32),
            pltpu.VMEM((views, 4 * n, LANES), f32),
            dma((plan.nx,)),
            dma((lights, cells_x)),
            dma((lights,)),
            dma((lights,)),
            dma((5,)),
            dma((plan.nx, plan.groups)),
            dma((views,)),
        ],
        compiler_params=pltpu.CompilerParams(
            collective_id=0, has_side_effects=True
        ),
    )(density, occupied, view_sign, transfer, absorb, light_in)


def solution(mesh):
    in_specs = (
        P("light", "view", None),
        P("light", "view", None),
        P(),
        P(),
        P(),
        P(None, "view", None),
    )
    out_specs = P(None, ("light", "view"))
    return jax.shard_map(body, mesh=mesh, in_specs=in_specs, out_specs=out_specs, check_vma=False)
```

```python
import functools

import jax
import jax.numpy as jnp
from jax import lax
from jax.experimental import pallas as pl
from jax.experimental.pallas import tpu as pltpu
from jax.sharding import PartitionSpec as P

LANES = 128
HALF = LANES // 2
MESH = pl.DeviceIdType.MESH


class Plan:
    def __init__(self, lights, views, cells_x, cells_y, columns, bricks):
        self.lights, self.views = lights, views
        self.cx, self.cy = cells_x, cells_y
        self.nx, self.ny = cells_x * lights, cells_y * views
        self.tiles = columns // LANES
        self.rows = self.tiles // lights
        self.win_tiles = self.rows + (2 if lights > 2 else 1)
        self.width = self.win_tiles * LANES
        self.piece_rows = cells_x * self.tiles // views
        self.groups = self.rows // self.piece_rows
        self.per_layer = self.tiles // self.piece_rows
        self.tiles_per_brick = self.tiles // bricks
        self.bricks = bricks

    def window(self, light):
        return jnp.clip(light * self.rows - 1, 0, self.tiles - self.win_tiles)


def cubic(coeffs, x):
    return coeffs[0] + x * (coeffs[1] + x * (coeffs[2] + x * coeffs[3]))


def kernel(
    plan,
    density,
    occupied_hbm,
    view_sign_hbm,
    transfer_hbm,
    absorb_hbm,
    light_in,
    out,
    occupied,
    view_sign,
    transfer,
    absorb,
    wbuf,
    lbuf,
    occ,
    dens,
    slope_z,
    transmit,
    lit,
    base,
    front,
    edge_front,
    edge_prod,
    image,
    recv,
    dsem,
    dsend,
    osem,
    osend,
    lsem,
    isend,
    rsem,
):
    lights, views, rows, cy = plan.lights, plan.views, plan.rows, plan.cy
    me_l = lax.axis_index("light")
    me_v = lax.axis_index("view")
    win = plan.window(me_l)
    off = me_l * rows - win
    slab_of_me = ((me_v * plan.piece_rows) % plan.tiles) // rows

    small_copies = [
        pltpu.make_async_copy(src, dst, lsem.at[i])
        for i, (src, dst) in enumerate(
            (
                (occupied_hbm, occupied),
                (view_sign_hbm, view_sign),
                (transfer_hbm, transfer),
                (absorb_hbm, absorb),
            )
        )
    ]
    for copy in small_copies:
        copy.start()

    barrier = pltpu.get_barrier_semaphore()
    for k in range(1, lights):
        pl.semaphore_signal(
            barrier, inc=1, device_id={"light": (me_l + k) % lights, "view": me_v}, device_id_type=MESH
        )

    def greet(v, carry):
        @pl.when(jnp.logical_or(v != me_v, slab_of_me != me_l))
        def _():
            pl.semaphore_signal(
                barrier, inc=1, device_id={"light": slab_of_me, "view": v}, device_id_type=MESH
            )

        return carry

    lax.fori_loop(0, views, greet, 0)

    def columns_of(light):
        return pl.ds(pl.multiple_of(plan.window(light) * LANES, LANES), plan.width)

    for i in range(plan.cx):
        layer = me_l * plan.cx + i
        pltpu.make_async_copy(
            density.at[i, :, columns_of(me_l)], wbuf.at[layer], dsem.at[layer]
        ).start()
    light_copy = pltpu.make_async_copy(light_in.at[:, :, columns_of(me_l)], lbuf, lsem.at[4])
    light_copy.start()

    for copy in small_copies:
        copy.wait()
    for k in range(plan.bricks):
        value = jnp.full((plan.tiles_per_brick, LANES), occupied[0, 0, k].astype(jnp.float32))
        occ[me_l, k * plan.tiles_per_brick : (k + 1) * plan.tiles_per_brick, :] = value

    @pl.when(slab_of_me == me_l)
    def _():
        pl.semaphore_wait(barrier, lights - 1 + views - 1)

    @pl.when(slab_of_me != me_l)
    def _():
        pl.semaphore_wait(barrier, lights - 1 + views)

    def occ_copy(k):
        return pltpu.make_async_remote_copy(
            src_ref=occ.at[me_l],
            dst_ref=occ.at[me_l],
            send_sem=osend.at[k],
            recv_sem=osem.at[me_l],
            device_id={"light": (me_l + k) % lights, "view": me_v},
            device_id_type=MESH,
        )

    def dens_copy(k, i):
        other = (me_l + k) % lights
        layer = me_l * plan.cx + i
        return pltpu.make_async_remote_copy(
            src_ref=density.at[i, :, columns_of(other)],
            dst_ref=wbuf.at[layer],
            send_sem=dsend.at[k, i],
            recv_sem=dsem.at[layer],
            device_id={"light": other, "view": me_v},
            device_id_type=MESH,
        )

    for k in range(1, lights):
        occ_copy(k).start()
    for i in range(plan.cx):
        for k in range(1, lights):
            dens_copy(k, i).start()

    core = (rows, LANES)
    lane = lax.broadcasted_iota(jnp.int32, core, 1)
    sub = lax.broadcasted_iota(jnp.int32, core, 0)
    first_lane, last_lane = lane == 0, lane == LANES - 1
    first_row, last_row = sub == 0, sub == rows - 1
    flat = (cy, LANES)
    flat_lane = lax.broadcasted_iota(jnp.int32, flat, 1)
    flat_first, flat_last = flat_lane == 0, flat_lane == LANES - 1
    flat_low = flat_lane < HALF
    sign = jnp.full(core, view_sign[0, 0])
    facing_back = sign < 0.0
    path_rate = (-2.0 / plan.ny) / jnp.abs(sign)
    rates = [absorb[c] * (-1.0 / plan.nx) for c in range(3)]
    ext_coeffs = [transfer[0, k] for k in range(4)]
    colour_coeffs = [[transfer[c, k] * 0.5 for k in range(4)] for c in (1, 2, 3)]
    has_left = jnp.where(me_l > 0, 1.0, 0.0)
    has_right = jnp.where(me_l < lights - 1, 1.0, 0.0)
    edge_tiles = [jnp.where(me_l == 0, rows - 1, 0)]
    if lights > 2:
        edge_tiles = [jnp.maximum(off - 1, 0), jnp.minimum(off + rows - 1, plan.win_tiles - 2)]
    seam_mask = jnp.where(flat_low, has_right, has_left)

    zeros = jnp.zeros((cy * rows, LANES), jnp.float32)
    dens[0] = zeros

    def tile_at(ref, lead, t):
        return ref[lead, :, pl.ds(pl.multiple_of(t * LANES, LANES), LANES)].astype(jnp.float32)

    def straddle(a, b):
        return pltpu.roll(jnp.where(flat_low, b, a), HALF, 1)

    def wait_layer(x):
        pltpu.make_async_copy(wbuf.at[x], wbuf.at[x], dsem.at[x]).wait()

    def spread(x):
        inside = jnp.where(x < plan.nx, 1.0, 0.0)
        layer = jnp.minimum(x, plan.nx - 1)
        tiles = [tile_at(wbuf, layer, jnp.maximum(off - 1, 0)) * has_left]
        tiles += [tile_at(wbuf, layer, off + t) for t in range(rows)]
        tiles += [tile_at(wbuf, layer, jnp.minimum(off + rows, plan.win_tiles - 1)) * has_right]
        for t in range(rows):
            here = tiles[t + 1]
            after = pltpu.roll(jnp.where(flat_first, tiles[t + 2], here), LANES - 1, 1)
            before = pltpu.roll(jnp.where(flat_last, tiles[t], here), 1, 1)
            dens[x + 1, pl.ds(t, cy, stride=rows), :] = here * inside
            slope_z[layer, pl.ds(t, cy, stride=rows), :] = after - before

    def wait_occ(block):
        @pl.when(block != me_l)
        def _():
            pltpu.make_async_copy(occ.at[block], occ.at[block], osem.at[block]).wait()

    def cross(x):
        layer = jnp.minimum(x, plan.nx - 1)
        block = layer // plan.cx
        seams = [[] for _ in range(3)]
        for e, t in enumerate(edge_tiles):
            cells = straddle(tile_at(wbuf, layer, t), tile_at(wbuf, layer, t + 1))
            held_a = occ[block, pl.ds(win + t, 1), :]
            held_b = occ[block, pl.ds(win + t + 1, 1), :]
            held = jnp.where(flat_low[:1], held_a, held_b)
            ext = jnp.log(1.0 + jnp.exp(cubic(ext_coeffs, cells))) * held
            for c in range(3):
                prod = edge_front[e, c] * jnp.exp(rates[c] * ext)
                seams[c].append(pltpu.roll(prod, HALF, 1))
                edge_front[e, c] = 0.5 * prod + 0.25 * (
                    pltpu.roll(prod, 1, 1) + pltpu.roll(prod, LANES - 1, 1)
                )
        for c in range(3):
            seam = seams[c][0]
            if len(edge_tiles) > 1:
                seam = jnp.where(flat_low, seams[c][1], seam)
            edge_prod[x % 2, c] = seam * seam_mask

    def cells_of(y):
        return slice(y * rows, (y + 1) * rows)

    def prepare(x):
        held = occ[x // plan.cx, pl.ds(pl.multiple_of(me_l * rows, rows), rows), :]

        def at(layer, y):
            return dens[layer, cells_of(y), :]

        passing = []
        for y in range(cy):
            ext = jnp.log(1.0 + jnp.exp(cubic(ext_coeffs, at(x + 1, y)))) * held
            passing.append(jnp.exp(path_rate * ext))
            for c in range(3):
                transmit[x, c, cells_of(y), :] = jnp.exp(rates[c] * ext)
        behind = [jnp.full(core, 0.5)]
        for y in reversed(range(1, cy)):
            behind.append(behind[-1] * passing[y])
        in_front = jnp.full(core, 0.5)
        ambient = [jnp.zeros(core, jnp.float32) for _ in range(3)]
        for y in range(cy):
            seen = jnp.where(facing_back, behind[cy - 1 - y], in_front) * (1.0 - passing[y])
            in_front = in_front * passing[y]
            d = at(x + 1, y)
            gx = at(x + 2, y) - at(x, y)
            gy = at(x + 1, min(y + 1, cy - 1)) - at(x + 1, max(y - 1, 0))
            gz = slope_z[x, cells_of(y), :]
            facing = (0.28 * gx + 0.126 * gy + 0.168 * gz) * lax.rsqrt(
                4.0 + gx * gx + gy * gy + gz * gz
            )
            shading = 0.65 + facing
            for c in range(3):
                coloured = seen * (1.0 + jnp.tanh(cubic(colour_coeffs[c], d)))
                ambient[c] = ambient[c] + coloured
                lit[x, c, cells_of(y), :] = coloured * shading
        for c in range(3):
            base[x, c] = 0.2 * ambient[c]
        base[x, 3] = 1.0 - 2.0 * in_front

    def shine(x):
        pixels = [base[x, c] for c in range(4)]
        for y in range(cy):
            for c in range(3):
                f = front[c, cells_of(y), :]
                pixels[c] = pixels[c] + f * lit[x, c, cells_of(y), :]
                prod = f * transmit[x, c, cells_of(y), :]
                seam = edge_prod[x % 2, c, y : y + 1, :]
                up = jnp.where(first_row, seam, pltpu.roll(prod, 1, 0))
                down = jnp.where(last_row, seam, pltpu.roll(prod, rows - 1, 0))
                before = pltpu.roll(jnp.where(last_lane, up, prod), 1, 1)
                after = pltpu.roll(jnp.where(first_lane, down, prod), LANES - 1, 1)
                front[c, cells_of(y), :] = 0.5 * prod + 0.25 * (before + after)
        n = plan.piece_rows
        for j in range(plan.groups):
            for c in range(4):
                image[x, j, c * n : (c + 1) * n, :] = pixels[c][j * n : (j + 1) * n, :]

    def send_layer(x):
        for j in range(plan.groups):
            send_piece(x, j, True)

    def send_piece(x, j, start):
        owner_l = x // plan.cx
        owner_v = (x % plan.cx) * plan.per_layer + me_l * plan.groups + j
        mine = jnp.logical_and(owner_l == me_l, owner_v == me_v)

        @pl.when(mine)
        def _():
            if start:
                pltpu.make_async_copy(image.at[x, j], recv.at[me_v], rsem.at[me_v]).start()

        @pl.when(jnp.logical_not(mine))
        def _():
            copy = pltpu.make_async_remote_copy(
                src_ref=image.at[x, j],
                dst_ref=recv.at[me_v],
                send_sem=isend.at[x, j],
                recv_sem=rsem.at[me_v],
                device_id={"light": owner_l, "view": owner_v},
                device_id_type=MESH,
            )
            if start:
                copy.start()
            else:
                copy.wait_send()

    start = jnp.where(me_l > 0, me_l * plan.cx + 1, 0)
    lead = jnp.where(me_l > 0, plan.nx - start, 0)

    light_copy.wait()
    for c in range(3):
        for t in range(rows):
            front[c, pl.ds(t, cy, stride=rows), :] = tile_at(lbuf, c, off + t)
        for e, t in enumerate(edge_tiles):
            edge_front[e, c] = straddle(tile_at(lbuf, c, t), tile_at(lbuf, c, t + 1))

    @pl.when(me_l > 0)
    def _():
        wait_layer(start - 1)
        spread(start - 1)

    wait_layer(start)
    spread(start)

    @pl.when(me_l == 0)
    def _():
        cross(0)

    def arrive(x):
        new = jnp.logical_and(x < plan.nx, jnp.logical_and(x != start, x != start - 1))

        @pl.when(new)
        def _():
            wait_layer(x)

        @pl.when(jnp.logical_and(new, x % plan.cx == 0))
        def _():
            wait_occ(x // plan.cx)

    def early(step, carry):
        x = start + step
        arrive(x + 1)
        spread(x + 1)
        prepare(x)
        return carry

    def both(step, carry):
        x = (start + step) % plan.nx

        @pl.when(jnp.logical_and(x == 0, step > 0))
        def _():
            arrive(0)
            spread(0)
            cross(0)

        arrive(x + 1)
        spread(x + 1)
        cross(x + 1)
        prepare(x)
        shine(x)
        send_layer(x)
        return carry

    def late(x, carry):
        cross(x + 1)
        shine(x)
        send_layer(x)
        return carry

    lax.fori_loop(0, lead, early, 0)
    lax.fori_loop(lead, plan.nx, both, 0)
    lax.fori_loop(plan.nx - lead, plan.nx, late, 0)

    n = plan.piece_rows
    small = (n, LANES)
    back = jnp.full(small, view_sign[0, 0]) < 0.0

    def merge(v, carry):
        pltpu.make_async_copy(recv.at[v], recv.at[v], rsem.at[v]).wait()
        through, acc = carry[0], carry[1:]
        passing = 1.0 - recv[v, 3 * n : 4 * n, :]
        weight = jnp.where(back, 1.0, through)
        keep = jnp.where(back, passing, 1.0)
        acc = [keep * acc[c] + weight * recv[v, c * n : (c + 1) * n, :] for c in range(3)]
        return (through * passing, *acc)

    zero = jnp.zeros(small, jnp.float32)
    merged = lax.fori_loop(0, views, merge, (jnp.ones(small, jnp.float32), zero, zero, zero))
    pixels = list(merged[1:]) + [1.0 - merged[0]]
    for c in range(4):
        for r in range(n):
            out[c : c + 1, r * LANES : (r + 1) * LANES] = pixels[c][r : r + 1, :]

    def finish(x, carry):
        for j in range(plan.groups):
            send_piece(x, j, False)
        return carry

    lax.fori_loop(0, plan.nx, finish, 0)
    for k in range(1, lights):
        occ_copy(k).wait_send()
        for i in range(plan.cx):
            dens_copy(k, i).wait_send()


def body(density, occupied, view_sign, transfer, absorb, light_in):
    cells_x, cells_y, columns = density.shape
    plan = Plan(
        lax.axis_size("light"), lax.axis_size("view"), cells_x, cells_y, columns, occupied.shape[2]
    )
    lights, views = plan.lights, plan.views
    n = plan.piece_rows
    edges = 2 if lights > 2 else 1
    f32 = jnp.float32
    hbm = pl.BlockSpec(memory_space=pl.ANY)
    dma = pltpu.SemaphoreType.DMA
    return pl.pallas_call(
        functools.partial(kernel, plan),
        out_shape=jax.ShapeDtypeStruct((4, n * LANES), f32),
        in_specs=[hbm] * 6,
        out_specs=pl.BlockSpec(memory_space=pltpu.VMEM),
        scratch_shapes=[
            pltpu.SMEM(occupied.shape, occupied.dtype),
            pltpu.SMEM((1, 1), f32),
            pltpu.SMEM(transfer.shape, f32),
            pltpu.SMEM(absorb.shape, f32),
            pltpu.VMEM((plan.nx, cells_y, plan.width), density.dtype),
            pltpu.VMEM((3, cells_y, plan.width), f32),
            pltpu.VMEM((lights, plan.tiles, LANES), f32),
            pltpu.VMEM((plan.nx + 2, cells_y * plan.rows, LANES), f32),
            pltpu.VMEM((plan.nx, cells_y * plan.rows, LANES), f32),
            pltpu.VMEM((plan.nx, 3, cells_y * plan.rows, LANES), f32),
            pltpu.VMEM((plan.nx, 3, cells_y * plan.rows, LANES), f32),
            pltpu.VMEM((plan.nx, 4, plan.rows, LANES), f32),
            pltpu.VMEM((3, cells_y * plan.rows, LANES), f32),
            pltpu.VMEM((edges, 3, cells_y, LANES), f32),
            pltpu.VMEM((2, 3, cells_y, LANES), f32),
            pltpu.VMEM((plan.nx, plan.groups, 4 * n, LANES), f32),
            pltpu.VMEM((views, 4 * n, LANES), f32),
            dma((plan.nx,)),
            dma((lights, cells_x)),
            dma((lights,)),
            dma((lights,)),
            dma((5,)),
            dma((plan.nx, plan.groups)),
            dma((views,)),
        ],
        compiler_params=pltpu.CompilerParams(
            collective_id=0, has_side_effects=True
        ),
    )(density, occupied, view_sign.reshape(1, 1), transfer, absorb, light_in)


def solution(mesh):
    in_specs = (
        P("light", "view", None),
        P("light", "view", None),
        P(),
        P(),
        P(),
        P(None, "view", None),
    )
    out_specs = P(None, ("light", "view"))
    return jax.shard_map(body, mesh=mesh, in_specs=in_specs, out_specs=out_specs, check_vma=False)
```

```python
import functools

import jax
import jax.numpy as jnp
from jax import lax
from jax.experimental import pallas as pl
from jax.experimental.pallas import tpu as pltpu
from jax.sharding import PartitionSpec as P

LANES = 128
MESH = pl.DeviceIdType.MESH


class Plan:
    def __init__(self, lights, views, cells_x, cells_y, columns, bricks):
        self.lights, self.views = lights, views
        self.cx, self.cy = cells_x, cells_y
        self.nx, self.ny = cells_x * lights, cells_y * views
        self.tiles = columns // LANES
        self.rows = self.tiles // lights
        self.win_tiles = self.rows + (2 if lights > 2 else 1)
        self.width = self.win_tiles * LANES
        self.piece_rows = cells_x * self.tiles // views
        self.groups = self.rows // self.piece_rows
        self.per_layer = self.tiles // self.piece_rows
        self.tiles_per_brick = self.tiles // bricks
        self.bricks = bricks

    def window(self, light):
        return jnp.clip(light * self.rows - 1, 0, self.tiles - self.win_tiles)


def cubic(coeffs, x):
    return coeffs[0] + x * (coeffs[1] + x * (coeffs[2] + x * coeffs[3]))


def kernel(
    plan,
    density,
    occupied_hbm,
    view_sign_hbm,
    transfer_hbm,
    absorb_hbm,
    light_in,
    out,
    occupied,
    view_sign,
    transfer,
    absorb,
    wbuf,
    lbuf,
    occ,
    exts,
    transmit,
    lit,
    base,
    column,
    front,
    image,
    recv,
    dsem,
    dsend,
    osem,
    osend,
    lsem,
    isend,
    rsem,
):
    lights, views, rows, cy = plan.lights, plan.views, plan.rows, plan.cy
    me_l = lax.axis_index("light")
    me_v = lax.axis_index("view")
    win = plan.window(me_l)
    off = me_l * rows - win
    slab_of_me = ((me_v * plan.piece_rows) % plan.tiles) // rows

    small_copies = [
        pltpu.make_async_copy(src, dst, lsem.at[i])
        for i, (src, dst) in enumerate(
            (
                (occupied_hbm, occupied),
                (view_sign_hbm, view_sign),
                (transfer_hbm, transfer),
                (absorb_hbm, absorb),
            )
        )
    ]
    for copy in small_copies:
        copy.start()

    barrier = pltpu.get_barrier_semaphore()
    for k in range(1, lights):
        pl.semaphore_signal(
            barrier, inc=1, device_id={"light": (me_l + k) % lights, "view": me_v}, device_id_type=MESH
        )

    def greet(v, carry):
        @pl.when(jnp.logical_or(v != me_v, slab_of_me != me_l))
        def _():
            pl.semaphore_signal(
                barrier, inc=1, device_id={"light": slab_of_me, "view": v}, device_id_type=MESH
            )

        return carry

    lax.fori_loop(0, views, greet, 0)

    def columns_of(light):
        return pl.ds(pl.multiple_of(plan.window(light) * LANES, LANES), plan.width)

    for i in range(plan.cx):
        layer = me_l * plan.cx + i
        pltpu.make_async_copy(
            density.at[i, :, columns_of(me_l)], wbuf.at[layer + 1], dsem.at[layer]
        ).start()
    light_copy = pltpu.make_async_copy(light_in.at[:, :, columns_of(me_l)], lbuf, lsem.at[4])
    light_copy.start()

    for copy in small_copies:
        copy.wait()
    for k in range(plan.bricks):
        value = jnp.full((plan.tiles_per_brick, LANES), occupied[0, 0, k].astype(jnp.float32))
        occ[me_l, k * plan.tiles_per_brick : (k + 1) * plan.tiles_per_brick, :] = value

    @pl.when(slab_of_me == me_l)
    def _():
        pl.semaphore_wait(barrier, lights - 1 + views - 1)

    @pl.when(slab_of_me != me_l)
    def _():
        pl.semaphore_wait(barrier, lights - 1 + views)

    def occ_copy(k):
        return pltpu.make_async_remote_copy(
            src_ref=occ.at[me_l],
            dst_ref=occ.at[me_l],
            send_sem=osend.at[k],
            recv_sem=osem.at[me_l],
            device_id={"light": (me_l + k) % lights, "view": me_v},
            device_id_type=MESH,
        )

    def dens_copy(k, i):
        other = (me_l + k) % lights
        layer = me_l * plan.cx + i
        return pltpu.make_async_remote_copy(
            src_ref=density.at[i, :, columns_of(other)],
            dst_ref=wbuf.at[layer + 1],
            send_sem=dsend.at[k, i],
            recv_sem=dsem.at[layer],
            device_id={"light": other, "view": me_v},
            device_id_type=MESH,
        )

    for k in range(1, lights):
        occ_copy(k).start()
    for i in range(plan.cx):
        for k in range(1, lights):
            dens_copy(k, i).start()

    tile_shape = (cy, LANES)
    lane = lax.broadcasted_iota(jnp.int32, tile_shape, 1)
    first_lane, last_lane = lane == 0, lane == LANES - 1
    sign = jnp.full(tile_shape, view_sign[0, 0])
    path_rate = (-2.0 / plan.ny) / jnp.abs(sign)
    rates = [absorb[c] * (-1.0 / plan.nx) for c in range(3)]
    ext_coeffs = [transfer[0, k] for k in range(4)]
    colour_coeffs = [[transfer[c, k] * 0.5 for k in range(4)] for c in (1, 2, 3)]
    has_left = jnp.where(me_l > 0, 1.0, 0.0)
    has_right = jnp.where(me_l < lights - 1, 1.0, 0.0)

    to = lax.broadcasted_iota(jnp.int32, (cy, cy), 0)
    of = lax.broadcasted_iota(jnp.int32, (cy, cy), 1)
    after_y = (of == jnp.minimum(to + 1, cy - 1)).astype(jnp.float32)
    before_y = (of == jnp.maximum(to - 1, 0)).astype(jnp.float32)
    slope_y = (after_y - before_y).astype(jnp.bfloat16)
    to = lax.broadcasted_iota(jnp.int32, (cy + 8, 2 * cy), 0)
    of = lax.broadcasted_iota(jnp.int32, (cy + 8, 2 * cy), 1) % cy
    one, none = jnp.ones(to.shape, jnp.float32), jnp.zeros(to.shape, jnp.float32)
    near_first = jnp.where(of < to, one, none)
    near_last = jnp.where(of > to, one, none)
    sign_wide = jnp.full(to.shape, view_sign[0, 0])
    in_front = jnp.where(sign_wide < 0.0, near_last, near_first)
    in_front = jnp.where(to >= cy, one, in_front).astype(jnp.bfloat16)

    blank = jnp.zeros((cy, plan.width), wbuf.dtype)
    wbuf[0] = blank
    wbuf[plan.nx + 1] = blank

    def tile_at(ref, lead, t):
        return ref[lead, :, pl.ds(pl.multiple_of(t * LANES, LANES), LANES)].astype(jnp.float32)

    def next_to(left, here, right):
        before = pltpu.roll(jnp.where(last_lane, left, here), 1, 1)
        after = pltpu.roll(jnp.where(first_lane, right, here), LANES - 1, 1)
        return before, after

    def wait_layer(x):
        pltpu.make_async_copy(wbuf.at[x + 1], wbuf.at[x + 1], dsem.at[x]).wait()

    def wait_occ(block):
        @pl.when(block != me_l)
        def _():
            pltpu.make_async_copy(occ.at[block], occ.at[block], osem.at[block]).wait()

    def prepare(x):
        block = x // plan.cx
        for t in range(plan.win_tiles):
            held = occ[block, pl.ds(win + t, 1), :]
            cells = tile_at(wbuf, x + 1, t)
            ext = jnp.log(1.0 + jnp.exp(cubic(ext_coeffs, cells))) * held
            exts[t] = ext
            for c in range(3):
                transmit[x, c, t] = jnp.exp(rates[c] * ext)
        depths = [path_rate * exts[off + t] for t in range(rows)]
        high = [depth.astype(jnp.bfloat16) for depth in depths]
        low = [
            (depth - h.astype(jnp.float32)).astype(jnp.bfloat16) for depth, h in zip(depths, high)
        ]
        stacked = jnp.concatenate(
            [jnp.concatenate(high, axis=1), jnp.concatenate(low, axis=1)], axis=0
        )
        sums = jnp.dot(in_front, stacked, preferred_element_type=jnp.float32)
        own = wbuf[x + 1, :, pl.ds(pl.multiple_of(off * LANES, LANES), rows * LANES)]
        grad_y = jnp.dot(slope_y, own, preferred_element_type=jnp.float32)
        tiles = [tile_at(wbuf, x + 1, jnp.maximum(off - 1, 0)) * has_left]
        tiles += [tile_at(wbuf, x + 1, off + t) for t in range(rows)]
        tiles += [tile_at(wbuf, x + 1, jnp.minimum(off + rows, plan.win_tiles - 1)) * has_right]
        for t in range(rows):
            part = slice(t * LANES, (t + 1) * LANES)
            seen = jnp.exp(sums[:cy, part]) * (1.0 - jnp.exp(depths[t]))
            d = tiles[t + 1]
            before, after = next_to(tiles[t], d, tiles[t + 2])
            gx = tile_at(wbuf, x + 2, off + t) - tile_at(wbuf, x, off + t)
            gy = grad_y[:, part]
            gz = after - before
            facing = (0.14 * gx + 0.063 * gy + 0.084 * gz) * lax.rsqrt(
                4.0 + gx * gx + gy * gy + gz * gz
            )
            shading = 0.325 + facing
            for c in range(3):
                coloured = seen * (1.0 + jnp.tanh(cubic(colour_coeffs[c], d)))
                lit[x, c, t] = coloured * shading
                base[x, c, t * 8 : (t + 1) * 8, :] = 0.1 * sum(
                    coloured[k : k + 8] for k in range(0, cy, 8)
                )
            base[x, 3, t * 8 : (t + 1) * 8, :] = 1.0 - jnp.exp(sums[cy:, part])

    def shine(x):
        pixels = []
        for c in range(3):
            for t in range(rows):
                share = front[c, off + t] * lit[x, c, t]
                column[c, t * 8 : (t + 1) * 8, :] = base[x, c, t * 8 : (t + 1) * 8, :] + sum(
                    share[k : k + 8] for k in range(0, cy, 8)
                )
            prods = [front[c, t] * transmit[x, c, t] for t in range(plan.win_tiles)]
            outside = jnp.zeros(tile_shape, jnp.float32)
            prods = [outside] + prods + [outside]
            for t in range(plan.win_tiles):
                before, after = next_to(prods[t], prods[t + 1], prods[t + 2])
                front[c, t] = 0.5 * prods[t + 1] + 0.25 * (before + after)
        for c in range(3):
            pixels.append(sum(column[c, pl.ds(r, rows, stride=8), :] for r in range(8)))
        pixels.append(base[x, 3, pl.ds(0, rows, stride=8), :])
        n = plan.piece_rows
        for j in range(plan.groups):
            for c in range(4):
                image[x, j, c * n : (c + 1) * n, :] = pixels[c][j * n : (j + 1) * n, :]

    def send_layer(x):
        for j in range(plan.groups):
            send_piece(x, j, True)

    def send_piece(x, j, start):
        owner_l = x // plan.cx
        owner_v = (x % plan.cx) * plan.per_layer + me_l * plan.groups + j
        mine = jnp.logical_and(owner_l == me_l, owner_v == me_v)

        @pl.when(mine)
        def _():
            if start:
                pltpu.make_async_copy(image.at[x, j], recv.at[me_v], rsem.at[me_v]).start()

        @pl.when(jnp.logical_not(mine))
        def _():
            copy = pltpu.make_async_remote_copy(
                src_ref=image.at[x, j],
                dst_ref=recv.at[me_v],
                send_sem=isend.at[x, j],
                recv_sem=rsem.at[me_v],
                device_id={"light": owner_l, "view": owner_v},
                device_id_type=MESH,
            )
            if start:
                copy.start()
            else:
                copy.wait_send()

    start = jnp.where(me_l > 0, me_l * plan.cx + 1, 0)
    lead = jnp.where(me_l > 0, plan.nx - start, 0)

    light_copy.wait()
    for c in range(3):
        for t in range(plan.win_tiles):
            front[c, t] = lbuf[c, :, t * LANES : (t + 1) * LANES]

    @pl.when(me_l > 0)
    def _():
        wait_layer(start - 1)

    wait_layer(start)

    def arrive(x):
        new = jnp.logical_and(x < plan.nx, jnp.logical_and(x != start, x != start - 1))

        @pl.when(new)
        def _():
            wait_layer(x)

        @pl.when(jnp.logical_and(new, x % plan.cx == 0))
        def _():
            wait_occ(x // plan.cx)

    def early(step, carry):
        x = start + step
        arrive(x + 1)
        prepare(x)
        return carry

    def both(step, carry):
        x = (start + step) % plan.nx

        @pl.when(jnp.logical_and(x == 0, step > 0))
        def _():
            arrive(0)

        arrive(x + 1)
        prepare(x)
        shine(x)
        send_layer(x)
        return carry

    def late(x, carry):
        shine(x)
        send_layer(x)
        return carry

    lax.fori_loop(0, lead, early, 0)
    lax.fori_loop(lead, plan.nx, both, 0)
    lax.fori_loop(plan.nx - lead, plan.nx, late, 0)

    n = plan.piece_rows
    small = (n, LANES)
    back = jnp.full(small, view_sign[0, 0]) < 0.0

    def merge(v, carry):
        pltpu.make_async_copy(recv.at[v], recv.at[v], rsem.at[v]).wait()
        through, acc = carry[0], carry[1:]
        passing = 1.0 - recv[v, 3 * n : 4 * n, :]
        weight = jnp.where(back, 1.0, through)
        keep = jnp.where(back, passing, 1.0)
        acc = [keep * acc[c] + weight * recv[v, c * n : (c + 1) * n, :] for c in range(3)]
        return (through * passing, *acc)

    zero = jnp.zeros(small, jnp.float32)
    merged = lax.fori_loop(0, views, merge, (jnp.ones(small, jnp.float32), zero, zero, zero))
    pixels = list(merged[1:]) + [1.0 - merged[0]]
    for c in range(4):
        for r in range(n):
            out[c : c + 1, r * LANES : (r + 1) * LANES] = pixels[c][r : r + 1, :]

    def finish(x, carry):
        for j in range(plan.groups):
            send_piece(x, j, False)
        return carry

    lax.fori_loop(0, plan.nx, finish, 0)
    for k in range(1, lights):
        occ_copy(k).wait_send()
        for i in range(plan.cx):
            dens_copy(k, i).wait_send()


def body(density, occupied, view_sign, transfer, absorb, light_in):
    cells_x, cells_y, columns = density.shape
    plan = Plan(
        lax.axis_size("light"), lax.axis_size("view"), cells_x, cells_y, columns, occupied.shape[2]
    )
    lights, views = plan.lights, plan.views
    n = plan.piece_rows
    f32 = jnp.float32
    hbm = pl.BlockSpec(memory_space=pl.ANY)
    dma = pltpu.SemaphoreType.DMA
    return pl.pallas_call(
        functools.partial(kernel, plan),
        out_shape=jax.ShapeDtypeStruct((4, n * LANES), f32),
        in_specs=[hbm] * 6,
        out_specs=pl.BlockSpec(memory_space=pltpu.VMEM),
        scratch_shapes=[
            pltpu.SMEM(occupied.shape, occupied.dtype),
            pltpu.SMEM((1, 1), f32),
            pltpu.SMEM(transfer.shape, f32),
            pltpu.SMEM(absorb.shape, f32),
            pltpu.VMEM((plan.nx + 2, cells_y, plan.width), density.dtype),
            pltpu.VMEM((3, cells_y, plan.width), f32),
            pltpu.VMEM((lights, plan.tiles, LANES), f32),
            pltpu.VMEM((plan.win_tiles, cells_y, LANES), f32),
            pltpu.VMEM((plan.nx, 3, plan.win_tiles, cells_y, LANES), f32),
            pltpu.VMEM((plan.nx, 3, plan.rows, cells_y, LANES), f32),
            pltpu.VMEM((plan.nx, 4, plan.rows * 8, LANES), f32),
            pltpu.VMEM((3, plan.rows * 8, LANES), f32),
            pltpu.VMEM((3, plan.win_tiles, cells_y, LANES), f32),
            pltpu.VMEM((plan.nx, plan.groups, 4 * n, LANES), f32),
            pltpu.VMEM((views, 4 * n, LANES), f32),
            dma((plan.nx,)),
            dma((lights, cells_x)),
            dma((lights,)),
            dma((lights,)),
            dma((5,)),
            dma((plan.nx, plan.groups)),
            dma((views,)),
        ],
        compiler_params=pltpu.CompilerParams(
            collective_id=0, has_side_effects=True
        ),
    )(density, occupied, view_sign.reshape(1, 1), transfer, absorb, light_in)


def solution(mesh):
    in_specs = (
        P("light", "view", None),
        P("light", "view", None),
        P(),
        P(),
        P(),
        P(None, "view", None),
    )
    out_specs = P(None, ("light", "view"))
    return jax.shard_map(body, mesh=mesh, in_specs=in_specs, out_specs=out_specs, check_vma=False)
```

```python
import functools

import jax
import jax.numpy as jnp
from jax import lax
from jax.experimental import pallas as pl
from jax.experimental.pallas import tpu as pltpu
from jax.sharding import PartitionSpec as P

LANES = 128
MESH = pl.DeviceIdType.MESH


class Plan:
    def __init__(self, lights, views, cells_x, cells_y, columns, bricks):
        self.lights, self.views = lights, views
        self.cx, self.cy = cells_x, cells_y
        self.nx, self.ny = cells_x * lights, cells_y * views
        self.tiles = columns // LANES
        self.rows = self.tiles // lights
        self.win_tiles = self.rows + (2 if lights > 2 else 1)
        self.width = self.win_tiles * LANES
        self.piece_rows = cells_x * self.tiles // views
        self.groups = self.rows // self.piece_rows
        self.per_layer = self.tiles // self.piece_rows
        self.tiles_per_brick = self.tiles // bricks
        self.bricks = bricks

    def window(self, light):
        return jnp.clip(light * self.rows - 1, 0, self.tiles - self.win_tiles)


def cubic(coeffs, x):
    return coeffs[0] + x * (coeffs[1] + x * (coeffs[2] + x * coeffs[3]))


def kernel(
    plan,
    density,
    occupied_hbm,
    view_sign_hbm,
    transfer_hbm,
    absorb_hbm,
    light_in,
    out,
    view_sign,
    transfer,
    absorb,
    bricks,
    wbuf,
    lbuf,
    occ,
    exts,
    transmit,
    lit,
    base,
    column,
    front,
    image,
    recv,
    dsem,
    dsend,
    osem,
    osend,
    lsem,
    isend,
    rsem,
):
    lights, views, rows, cy = plan.lights, plan.views, plan.rows, plan.cy
    me_l = lax.axis_index("light")
    me_v = lax.axis_index("view")
    win = plan.window(me_l)
    off = me_l * rows - win
    slab_of_me = ((me_v * plan.piece_rows) % plan.tiles) // rows

    small_copies = [
        pltpu.make_async_copy(src, dst, lsem.at[i])
        for i, (src, dst) in enumerate(
            (
                (view_sign_hbm, view_sign),
                (transfer_hbm, transfer),
                (absorb_hbm, absorb),
            )
        )
    ]
    for copy in small_copies:
        copy.start()

    barrier = pltpu.get_barrier_semaphore()
    for k in range(1, lights):
        pl.semaphore_signal(
            barrier, inc=1, device_id={"light": (me_l + k) % lights, "view": me_v}, device_id_type=MESH
        )

    def greet(v, carry):
        @pl.when(jnp.logical_or(v != me_v, slab_of_me != me_l))
        def _():
            pl.semaphore_signal(
                barrier, inc=1, device_id={"light": slab_of_me, "view": v}, device_id_type=MESH
            )

        return carry

    lax.fori_loop(0, views, greet, 0)

    def columns_of(light):
        return pl.ds(pl.multiple_of(plan.window(light) * LANES, LANES), plan.width)

    for i in range(plan.cx):
        layer = me_l * plan.cx + i
        pltpu.make_async_copy(
            density.at[i, :, columns_of(me_l)], wbuf.at[layer + 1], dsem.at[layer]
        ).start()
    light_copy = pltpu.make_async_copy(light_in.at[:, :, columns_of(me_l)], lbuf, lsem.at[4])
    light_copy.start()

    pltpu.make_async_copy(occupied_hbm.at[0], bricks.at[me_l], osem.at[me_l]).start()

    @pl.when(slab_of_me == me_l)
    def _():
        pl.semaphore_wait(barrier, lights - 1 + views - 1)

    @pl.when(slab_of_me != me_l)
    def _():
        pl.semaphore_wait(barrier, lights - 1 + views)

    def occ_copy(k):
        return pltpu.make_async_remote_copy(
            src_ref=occupied_hbm.at[0],
            dst_ref=bricks.at[me_l],
            send_sem=osend.at[k],
            recv_sem=osem.at[me_l],
            device_id={"light": (me_l + k) % lights, "view": me_v},
            device_id_type=MESH,
        )

    def dens_copy(k, i):
        other = (me_l + k) % lights
        layer = me_l * plan.cx + i
        return pltpu.make_async_remote_copy(
            src_ref=density.at[i, :, columns_of(other)],
            dst_ref=wbuf.at[layer + 1],
            send_sem=dsend.at[k, i],
            recv_sem=dsem.at[layer],
            device_id={"light": other, "view": me_v},
            device_id_type=MESH,
        )

    for k in range(1, lights):
        occ_copy(k).start()
    for i in range(plan.cx):
        for k in range(1, lights):
            dens_copy(k, i).start()

    for copy in small_copies:
        copy.wait()

    tile_shape = (cy, LANES)
    lane = lax.broadcasted_iota(jnp.int32, tile_shape, 1)
    first_lane, last_lane = lane == 0, lane == LANES - 1
    sign = jnp.full(tile_shape, view_sign[0, 0])
    path_rate = (-2.0 / plan.ny) / jnp.abs(sign)
    rates = [absorb[c] * (-1.0 / plan.nx) for c in range(3)]
    ext_coeffs = [transfer[0, k] for k in range(4)]
    colour_coeffs = [[transfer[c, k] * 0.5 for k in range(4)] for c in (1, 2, 3)]
    has_left = jnp.where(me_l > 0, 1.0, 0.0)
    has_right = jnp.where(me_l < lights - 1, 1.0, 0.0)

    to = lax.broadcasted_iota(jnp.int32, (cy, cy), 0)
    of = lax.broadcasted_iota(jnp.int32, (cy, cy), 1)
    after_y = (of == jnp.minimum(to + 1, cy - 1)).astype(jnp.float32)
    before_y = (of == jnp.maximum(to - 1, 0)).astype(jnp.float32)
    slope_y = (after_y - before_y).astype(jnp.bfloat16)
    to = lax.broadcasted_iota(jnp.int32, (cy + 8, 2 * cy), 0)
    of = lax.broadcasted_iota(jnp.int32, (cy + 8, 2 * cy), 1) % cy
    one, none = jnp.ones(to.shape, jnp.float32), jnp.zeros(to.shape, jnp.float32)
    near_first = jnp.where(of < to, one, none)
    near_last = jnp.where(of > to, one, none)
    sign_wide = jnp.full(to.shape, view_sign[0, 0])
    in_front = jnp.where(sign_wide < 0.0, near_last, near_first)
    in_front = jnp.where(to >= cy, one, in_front).astype(jnp.bfloat16)

    blank = jnp.zeros((cy, plan.width), wbuf.dtype)
    wbuf[0] = blank
    wbuf[plan.nx + 1] = blank

    def tile_at(ref, lead, t):
        return ref[lead, :, pl.ds(pl.multiple_of(t * LANES, LANES), LANES)].astype(jnp.float32)

    def next_to(left, here, right):
        before = pltpu.roll(jnp.where(last_lane, left, here), 1, 1)
        after = pltpu.roll(jnp.where(first_lane, right, here), LANES - 1, 1)
        return before, after

    def wait_layer(x):
        pltpu.make_async_copy(wbuf.at[x + 1], wbuf.at[x + 1], dsem.at[x]).wait()

    tile_of = lax.broadcasted_iota(jnp.int32, (plan.tiles, plan.bricks), 0)
    brick_of = lax.broadcasted_iota(jnp.int32, (plan.tiles, plan.bricks), 1)
    own_brick = tile_of // plan.tiles_per_brick == brick_of

    def wait_occ(block):
        pltpu.make_async_copy(bricks.at[block], bricks.at[block], osem.at[block]).wait()
        row = jnp.broadcast_to(bricks[block], own_brick.shape).astype(jnp.float32)
        held = jnp.sum(jnp.where(own_brick, row, 0.0), axis=1, keepdims=True)
        occ[block] = jnp.broadcast_to(held, (plan.tiles, LANES))

    def prepare(x):
        block = x // plan.cx
        for t in range(plan.win_tiles):
            held = occ[block, pl.ds(win + t, 1), :]
            cells = tile_at(wbuf, x + 1, t)
            ext = jnp.log(1.0 + jnp.exp(cubic(ext_coeffs, cells))) * held
            exts[t] = ext
            for c in range(3):
                transmit[x, c, t] = jnp.exp(rates[c] * ext)
        depths = [path_rate * exts[off + t] for t in range(rows)]
        high = [depth.astype(jnp.bfloat16) for depth in depths]
        low = [
            (depth - h.astype(jnp.float32)).astype(jnp.bfloat16) for depth, h in zip(depths, high)
        ]
        stacked = jnp.concatenate(
            [jnp.concatenate(high, axis=1), jnp.concatenate(low, axis=1)], axis=0
        )
        sums = jnp.dot(in_front, stacked, preferred_element_type=jnp.float32)
        own = wbuf[x + 1, :, pl.ds(pl.multiple_of(off * LANES, LANES), rows * LANES)]
        grad_y = jnp.dot(slope_y, own, preferred_element_type=jnp.float32)
        tiles = [tile_at(wbuf, x + 1, jnp.maximum(off - 1, 0)) * has_left]
        tiles += [tile_at(wbuf, x + 1, off + t) for t in range(rows)]
        tiles += [tile_at(wbuf, x + 1, jnp.minimum(off + rows, plan.win_tiles - 1)) * has_right]
        for t in range(rows):
            part = slice(t * LANES, (t + 1) * LANES)
            seen = jnp.exp(sums[:cy, part]) * (1.0 - jnp.exp(depths[t]))
            d = tiles[t + 1]
            before, after = next_to(tiles[t], d, tiles[t + 2])
            gx = tile_at(wbuf, x + 2, off + t) - tile_at(wbuf, x, off + t)
            gy = grad_y[:, part]
            gz = after - before
            facing = (0.14 * gx + 0.063 * gy + 0.084 * gz) * lax.rsqrt(
                4.0 + gx * gx + gy * gy + gz * gz
            )
            shading = 0.325 + facing
            for c in range(3):
                coloured = seen * (1.0 + jnp.tanh(cubic(colour_coeffs[c], d)))
                lit[x, c, t] = coloured * shading
                base[x, c, t * 8 : (t + 1) * 8, :] = 0.1 * sum(
                    coloured[k : k + 8] for k in range(0, cy, 8)
                )
            base[x, 3, t * 8 : (t + 1) * 8, :] = 1.0 - jnp.exp(sums[cy:, part])

    def shine(x):
        pixels = []
        for c in range(3):
            for t in range(rows):
                share = front[c, off + t] * lit[x, c, t]
                column[c, t * 8 : (t + 1) * 8, :] = base[x, c, t * 8 : (t + 1) * 8, :] + sum(
                    share[k : k + 8] for k in range(0, cy, 8)
                )
            prods = [front[c, t] * transmit[x, c, t] for t in range(plan.win_tiles)]
            outside = jnp.zeros(tile_shape, jnp.float32)
            prods = [outside] + prods + [outside]
            for t in range(plan.win_tiles):
                before, after = next_to(prods[t], prods[t + 1], prods[t + 2])
                front[c, t] = 0.5 * prods[t + 1] + 0.25 * (before + after)
        for c in range(3):
            pixels.append(sum(column[c, pl.ds(r, rows, stride=8), :] for r in range(8)))
        pixels.append(base[x, 3, pl.ds(0, rows, stride=8), :])
        n = plan.piece_rows
        for j in range(plan.groups):
            for c in range(4):
                image[x, j, c * n : (c + 1) * n, :] = pixels[c][j * n : (j + 1) * n, :]

    def send_layer(x):
        for j in range(plan.groups):
            send_piece(x, j, True)

    def send_piece(x, j, start):
        owner_l = x // plan.cx
        owner_v = (x % plan.cx) * plan.per_layer + me_l * plan.groups + j
        mine = jnp.logical_and(owner_l == me_l, owner_v == me_v)

        @pl.when(mine)
        def _():
            if start:
                pltpu.make_async_copy(image.at[x, j], recv.at[me_v], rsem.at[me_v]).start()

        @pl.when(jnp.logical_not(mine))
        def _():
            copy = pltpu.make_async_remote_copy(
                src_ref=image.at[x, j],
                dst_ref=recv.at[me_v],
                send_sem=isend.at[x, j],
                recv_sem=rsem.at[me_v],
                device_id={"light": owner_l, "view": owner_v},
                device_id_type=MESH,
            )
            if start:
                copy.start()
            else:
                copy.wait_send()

    start = jnp.where(me_l > 0, me_l * plan.cx + 1, 0)
    lead = jnp.where(me_l > 0, plan.nx - start, 0)

    light_copy.wait()
    for c in range(3):
        for t in range(plan.win_tiles):
            front[c, t] = lbuf[c, :, t * LANES : (t + 1) * LANES]

    @pl.when(me_l > 0)
    def _():
        wait_layer(start - 1)

    wait_layer(start)
    wait_occ(me_l)

    def arrive(x):
        new = jnp.logical_and(x < plan.nx, jnp.logical_and(x != start, x != start - 1))

        @pl.when(new)
        def _():
            wait_layer(x)

        @pl.when(jnp.logical_and(new, jnp.logical_and(x % plan.cx == 0, x // plan.cx != me_l)))
        def _():
            wait_occ(x // plan.cx)

    def early(step, carry):
        x = start + step
        arrive(x + 1)
        prepare(x)
        return carry

    def both(step, carry):
        x = (start + step) % plan.nx

        @pl.when(jnp.logical_and(x == 0, step > 0))
        def _():
            arrive(0)

        arrive(x + 1)
        prepare(x)
        shine(x)
        send_layer(x)
        return carry

    def late(x, carry):
        shine(x)
        send_layer(x)
        return carry

    lax.fori_loop(0, lead, early, 0)
    lax.fori_loop(lead, plan.nx, both, 0)
    lax.fori_loop(plan.nx - lead, plan.nx, late, 0)

    n = plan.piece_rows
    small = (n, LANES)
    back = jnp.full(small, view_sign[0, 0]) < 0.0

    def merge(v, carry):
        pltpu.make_async_copy(recv.at[v], recv.at[v], rsem.at[v]).wait()
        through, acc = carry[0], carry[1:]
        passing = 1.0 - recv[v, 3 * n : 4 * n, :]
        weight = jnp.where(back, 1.0, through)
        keep = jnp.where(back, passing, 1.0)
        acc = [keep * acc[c] + weight * recv[v, c * n : (c + 1) * n, :] for c in range(3)]
        return (through * passing, *acc)

    zero = jnp.zeros(small, jnp.float32)
    merged = lax.fori_loop(0, views, merge, (jnp.ones(small, jnp.float32), zero, zero, zero))
    pixels = list(merged[1:]) + [1.0 - merged[0]]
    for c in range(4):
        for r in range(n):
            out[c : c + 1, r * LANES : (r + 1) * LANES] = pixels[c][r : r + 1, :]

    def finish(x, carry):
        for j in range(plan.groups):
            send_piece(x, j, False)
        return carry

    lax.fori_loop(0, plan.nx, finish, 0)
    for k in range(1, lights):
        occ_copy(k).wait_send()
        for i in range(plan.cx):
            dens_copy(k, i).wait_send()


def body(density, occupied, view_sign, transfer, absorb, light_in):
    cells_x, cells_y, columns = density.shape
    plan = Plan(
        lax.axis_size("light"), lax.axis_size("view"), cells_x, cells_y, columns, occupied.shape[2]
    )
    lights, views = plan.lights, plan.views
    n = plan.piece_rows
    f32 = jnp.float32
    hbm = pl.BlockSpec(memory_space=pl.ANY)
    dma = pltpu.SemaphoreType.DMA
    return pl.pallas_call(
        functools.partial(kernel, plan),
        out_shape=jax.ShapeDtypeStruct((4, n * LANES), f32),
        in_specs=[hbm] * 6,
        out_specs=pl.BlockSpec(memory_space=pltpu.VMEM),
        scratch_shapes=[
            pltpu.SMEM((1, 1), f32),
            pltpu.SMEM(transfer.shape, f32),
            pltpu.SMEM(absorb.shape, f32),
            pltpu.VMEM((lights,) + occupied.shape[1:], occupied.dtype),
            pltpu.VMEM((plan.nx + 2, cells_y, plan.width), density.dtype),
            pltpu.VMEM((3, cells_y, plan.width), f32),
            pltpu.VMEM((lights, plan.tiles, LANES), f32),
            pltpu.VMEM((plan.win_tiles, cells_y, LANES), f32),
            pltpu.VMEM((plan.nx, 3, plan.win_tiles, cells_y, LANES), f32),
            pltpu.VMEM((plan.nx, 3, plan.rows, cells_y, LANES), f32),
            pltpu.VMEM((plan.nx, 4, plan.rows * 8, LANES), f32),
            pltpu.VMEM((3, plan.rows * 8, LANES), f32),
            pltpu.VMEM((3, plan.win_tiles, cells_y, LANES), f32),
            pltpu.VMEM((plan.nx, plan.groups, 4 * n, LANES), f32),
            pltpu.VMEM((views, 4 * n, LANES), f32),
            dma((plan.nx,)),
            dma((lights, cells_x)),
            dma((lights,)),
            dma((lights,)),
            dma((5,)),
            dma((plan.nx, plan.groups)),
            dma((views,)),
        ],
        compiler_params=pltpu.CompilerParams(
            collective_id=0, has_side_effects=True
        ),
    )(density, occupied, view_sign.reshape(1, 1), transfer, absorb, light_in)


def solution(mesh):
    in_specs = (
        P("light", "view", None),
        P("light", "view", None),
        P(),
        P(),
        P(),
        P(None, "view", None),
    )
    out_specs = P(None, ("light", "view"))
    return jax.shard_map(body, mesh=mesh, in_specs=in_specs, out_specs=out_specs, check_vma=False)
```

```python
import functools

import jax
import jax.numpy as jnp
from jax import lax
from jax.experimental import pallas as pl
from jax.experimental.pallas import tpu as pltpu
from jax.sharding import PartitionSpec as P

LANES = 128
MESH = pl.DeviceIdType.MESH


class Plan:
    def __init__(self, lights, views, cells_x, cells_y, columns, bricks):
        self.lights, self.views = lights, views
        self.cx, self.cy = cells_x, cells_y
        self.nx, self.ny = cells_x * lights, cells_y * views
        self.tiles = columns // LANES
        self.rows = self.tiles // lights
        self.win_tiles = self.rows + (2 if lights > 2 else 1)
        self.width = self.win_tiles * LANES
        self.piece_rows = cells_x * self.tiles // views
        self.groups = self.rows // self.piece_rows
        self.per_layer = self.tiles // self.piece_rows
        self.tiles_per_brick = self.tiles // bricks
        self.bricks = bricks

    def window(self, light):
        return jnp.clip(light * self.rows - 1, 0, self.tiles - self.win_tiles)


def cubic(coeffs, x):
    return coeffs[0] + x * (coeffs[1] + x * (coeffs[2] + x * coeffs[3]))


def kernel(
    plan,
    density,
    occupied_hbm,
    view_sign_hbm,
    transfer_hbm,
    absorb_hbm,
    light_in,
    out,
    view_sign,
    transfer,
    absorb,
    bricks,
    wbuf,
    lbuf,
    occ,
    transmit,
    lit,
    base,
    column,
    front,
    image,
    recv,
    dsem,
    dsend,
    osem,
    osend,
    lsem,
    isend,
    rsem,
):
    lights, views, rows, cy = plan.lights, plan.views, plan.rows, plan.cy
    me_l = lax.axis_index("light")
    me_v = lax.axis_index("view")
    win = plan.window(me_l)
    off = me_l * rows - win
    slab_of_me = ((me_v * plan.piece_rows) % plan.tiles) // rows

    small_copies = [
        pltpu.make_async_copy(src, dst, lsem.at[i])
        for i, (src, dst) in enumerate(
            (
                (view_sign_hbm, view_sign),
                (transfer_hbm, transfer),
                (absorb_hbm, absorb),
            )
        )
    ]
    for copy in small_copies:
        copy.start()

    barrier = pltpu.get_barrier_semaphore()
    for k in range(1, lights):
        pl.semaphore_signal(
            barrier, inc=1, device_id={"light": (me_l + k) % lights, "view": me_v}, device_id_type=MESH
        )

    def greet(v, carry):
        @pl.when(jnp.logical_or(v != me_v, slab_of_me != me_l))
        def _():
            pl.semaphore_signal(
                barrier, inc=1, device_id={"light": slab_of_me, "view": v}, device_id_type=MESH
            )

        return carry

    lax.fori_loop(0, views, greet, 0)

    def columns_of(light):
        return pl.ds(pl.multiple_of(plan.window(light) * LANES, LANES), plan.width)

    for i in range(plan.cx):
        layer = me_l * plan.cx + i
        pltpu.make_async_copy(
            density.at[i, :, columns_of(me_l)], wbuf.at[layer + 1], dsem.at[layer]
        ).start()
    light_copy = pltpu.make_async_copy(light_in.at[:, :, columns_of(me_l)], lbuf, lsem.at[4])
    light_copy.start()

    pltpu.make_async_copy(occupied_hbm.at[0], bricks.at[me_l], osem.at[me_l]).start()

    @pl.when(slab_of_me == me_l)
    def _():
        pl.semaphore_wait(barrier, lights - 1 + views - 1)

    @pl.when(slab_of_me != me_l)
    def _():
        pl.semaphore_wait(barrier, lights - 1 + views)

    def occ_copy(k):
        return pltpu.make_async_remote_copy(
            src_ref=occupied_hbm.at[0],
            dst_ref=bricks.at[me_l],
            send_sem=osend.at[k],
            recv_sem=osem.at[me_l],
            device_id={"light": (me_l + k) % lights, "view": me_v},
            device_id_type=MESH,
        )

    def dens_copy(k, i):
        other = (me_l + k) % lights
        layer = me_l * plan.cx + i
        return pltpu.make_async_remote_copy(
            src_ref=density.at[i, :, columns_of(other)],
            dst_ref=wbuf.at[layer + 1],
            send_sem=dsend.at[k, i],
            recv_sem=dsem.at[layer],
            device_id={"light": other, "view": me_v},
            device_id_type=MESH,
        )

    for k in range(1, lights):
        occ_copy(k).start()
    for i in range(plan.cx):
        for k in range(1, lights):
            dens_copy(k, i).start()

    for copy in small_copies:
        copy.wait()

    tile_shape = (cy, LANES)
    lane = lax.broadcasted_iota(jnp.int32, tile_shape, 1)
    first_lane, last_lane = lane == 0, lane == LANES - 1
    sign = jnp.full(tile_shape, view_sign[0, 0])
    path_rate = (-2.0 / plan.ny) / jnp.abs(sign)
    rates = [absorb[c] * (-1.0 / plan.nx) for c in range(3)]
    ext_coeffs = [transfer[0, k] for k in range(4)]
    colour_coeffs = [[transfer[c, k] * 0.5 for k in range(4)] for c in (1, 2, 3)]
    has_left = jnp.where(me_l > 0, 1.0, 0.0)
    has_right = jnp.where(me_l < lights - 1, 1.0, 0.0)

    to = lax.broadcasted_iota(jnp.int32, (cy, cy), 0)
    of = lax.broadcasted_iota(jnp.int32, (cy, cy), 1)
    after_y = (of == jnp.minimum(to + 1, cy - 1)).astype(jnp.float32)
    before_y = (of == jnp.maximum(to - 1, 0)).astype(jnp.float32)
    slope_y = (after_y - before_y).astype(jnp.bfloat16)
    to = lax.broadcasted_iota(jnp.int32, (cy + 8, 2 * cy), 0)
    of = lax.broadcasted_iota(jnp.int32, (cy + 8, 2 * cy), 1) % cy
    one, none = jnp.ones(to.shape, jnp.float32), jnp.zeros(to.shape, jnp.float32)
    near_first = jnp.where(of < to, one, none)
    near_last = jnp.where(of > to, one, none)
    sign_wide = jnp.full(to.shape, view_sign[0, 0])
    in_front = jnp.where(sign_wide < 0.0, near_last, near_first)
    in_front = jnp.where(to >= cy, one, in_front).astype(jnp.bfloat16)

    blank = jnp.zeros((cy, plan.width), wbuf.dtype)
    wbuf[0] = blank
    wbuf[plan.nx + 1] = blank

    places = [off + t for t in range(rows)]
    if lights == 2:
        places += [jnp.where(me_l == 0, rows, 0)]
        halo_masks = [jnp.where(last_lane, has_left, jnp.where(first_lane, has_right, 1.0))]
    else:
        places += [jnp.minimum(off + rows, plan.win_tiles - 1), jnp.maximum(off - 1, 0)]
        halo_masks = [has_right, has_left]

    def tile_at(ref, lead, t):
        return ref[lead, :, pl.ds(pl.multiple_of(t * LANES, LANES), LANES)].astype(jnp.float32)

    def next_to(left, here, right):
        before = pltpu.roll(jnp.where(last_lane, left, here), 1, 1)
        after = pltpu.roll(jnp.where(first_lane, right, here), LANES - 1, 1)
        return before, after

    def wait_layer(x):
        pltpu.make_async_copy(wbuf.at[x + 1], wbuf.at[x + 1], dsem.at[x]).wait()

    tile_of = lax.broadcasted_iota(jnp.int32, (plan.tiles, plan.bricks), 0)
    brick_of = lax.broadcasted_iota(jnp.int32, (plan.tiles, plan.bricks), 1)
    own_brick = tile_of // plan.tiles_per_brick == brick_of

    def wait_occ(block):
        pltpu.make_async_copy(bricks.at[block], bricks.at[block], osem.at[block]).wait()
        row = jnp.broadcast_to(bricks[block], own_brick.shape).astype(jnp.float32)
        held = jnp.sum(jnp.where(own_brick, row, 0.0), axis=1, keepdims=True)
        occ[block] = jnp.broadcast_to(held, (plan.tiles, LANES))

    def prepare(x):
        block = x // plan.cx
        depths = []
        for t, place in enumerate(places):
            held = occ[block, pl.ds(win + place, 1), :]
            cells = tile_at(wbuf, x + 1, place)
            ext = jnp.log(1.0 + jnp.exp(cubic(ext_coeffs, cells))) * held
            if t < rows:
                depths.append(path_rate * ext)
            for c in range(3):
                through = jnp.exp(rates[c] * ext)
                transmit[x, c, t] = through if t < rows else through * halo_masks[t - rows]
        high = [depth.astype(jnp.bfloat16) for depth in depths]
        low = [
            (depth - h.astype(jnp.float32)).astype(jnp.bfloat16) for depth, h in zip(depths, high)
        ]
        stacked = jnp.concatenate(
            [jnp.concatenate(high, axis=1), jnp.concatenate(low, axis=1)], axis=0
        )
        sums = jnp.dot(in_front, stacked, preferred_element_type=jnp.float32)
        own = wbuf[x + 1, :, pl.ds(pl.multiple_of(off * LANES, LANES), rows * LANES)]
        grad_y = jnp.dot(slope_y, own, preferred_element_type=jnp.float32)
        tiles = [tile_at(wbuf, x + 1, jnp.maximum(off - 1, 0)) * has_left]
        tiles += [tile_at(wbuf, x + 1, off + t) for t in range(rows)]
        tiles += [tile_at(wbuf, x + 1, jnp.minimum(off + rows, plan.win_tiles - 1)) * has_right]
        for t in range(rows):
            part = slice(t * LANES, (t + 1) * LANES)
            seen = jnp.exp(sums[:cy, part]) * (1.0 - jnp.exp(depths[t]))
            d = tiles[t + 1]
            before, after = next_to(tiles[t], d, tiles[t + 2])
            gx = tile_at(wbuf, x + 2, off + t) - tile_at(wbuf, x, off + t)
            gy = grad_y[:, part]
            gz = after - before
            facing = (0.14 * gx + 0.063 * gy + 0.084 * gz) * lax.rsqrt(
                4.0 + gx * gx + gy * gy + gz * gz
            )
            shading = 0.325 + facing
            for c in range(3):
                coloured = seen * (1.0 + jnp.tanh(cubic(colour_coeffs[c], d)))
                lit[x, c, t] = coloured * shading
                base[x, c, t * 8 : (t + 1) * 8, :] = 0.1 * sum(
                    coloured[k : k + 8] for k in range(0, cy, 8)
                )
            base[x, 3, t * 8 : (t + 1) * 8, :] = 1.0 - jnp.exp(sums[cy:, part])

    def shine(x):
        pixels = []
        for c in range(3):
            for t in range(rows):
                share = front[c, t] * lit[x, c, t]
                column[c, t * 8 : (t + 1) * 8, :] = base[x, c, t * 8 : (t + 1) * 8, :] + sum(
                    share[k : k + 8] for k in range(0, cy, 8)
                )
            prods = [front[c, t] * transmit[x, c, t] for t in range(plan.win_tiles)]
            for t in range(plan.win_tiles):
                before, after = next_to(
                    prods[t - 1], prods[t], prods[(t + 1) % plan.win_tiles]
                )
                front[c, t] = 0.5 * prods[t] + 0.25 * (before + after)
        for c in range(3):
            pixels.append(sum(column[c, pl.ds(r, rows, stride=8), :] for r in range(8)))
        pixels.append(base[x, 3, pl.ds(0, rows, stride=8), :])
        n = plan.piece_rows
        for j in range(plan.groups):
            for c in range(4):
                image[x, j, c * n : (c + 1) * n, :] = pixels[c][j * n : (j + 1) * n, :]

    def send_layer(x):
        for j in range(plan.groups):
            send_piece(x, j, True)

    def send_piece(x, j, start):
        owner_l = x // plan.cx
        owner_v = (x % plan.cx) * plan.per_layer + me_l * plan.groups + j
        mine = jnp.logical_and(owner_l == me_l, owner_v == me_v)

        @pl.when(mine)
        def _():
            if start:
                pltpu.make_async_copy(image.at[x, j], recv.at[me_v], rsem.at[me_v]).start()

        @pl.when(jnp.logical_not(mine))
        def _():
            copy = pltpu.make_async_remote_copy(
                src_ref=image.at[x, j],
                dst_ref=recv.at[me_v],
                send_sem=isend.at[x, j],
                recv_sem=rsem.at[me_v],
                device_id={"light": owner_l, "view": owner_v},
                device_id_type=MESH,
            )
            if start:
                copy.start()
            else:
                copy.wait_send()

    start = jnp.where(me_l > 0, me_l * plan.cx + 1, 0)
    lead = jnp.where(me_l > 0, plan.nx - start, 0)

    light_copy.wait()
    for c in range(3):
        for t, place in enumerate(places):
            front[c, t] = tile_at(lbuf, c, place)

    @pl.when(me_l > 0)
    def _():
        wait_layer(start - 1)

    wait_layer(start)
    wait_occ(me_l)

    def arrive(x):
        new = jnp.logical_and(x < plan.nx, jnp.logical_and(x != start, x != start - 1))

        @pl.when(new)
        def _():
            wait_layer(x)

        @pl.when(jnp.logical_and(new, jnp.logical_and(x % plan.cx == 0, x // plan.cx != me_l)))
        def _():
            wait_occ(x // plan.cx)

    def early(step, carry):
        x = start + step
        arrive(x + 1)
        prepare(x)
        return carry

    def both(step, carry):
        x = (start + step) % plan.nx

        @pl.when(jnp.logical_and(x == 0, step > 0))
        def _():
            arrive(0)

        arrive(x + 1)
        prepare(x)
        shine(x)
        send_layer(x)
        return carry

    def late(x, carry):
        shine(x)
        send_layer(x)
        return carry

    lax.fori_loop(0, lead, early, 0)
    lax.fori_loop(lead, plan.nx, both, 0)
    lax.fori_loop(plan.nx - lead, plan.nx, late, 0)

    n = plan.piece_rows
    small = (n, LANES)
    back = jnp.full(small, view_sign[0, 0]) < 0.0

    def merge(v, carry):
        pltpu.make_async_copy(recv.at[v], recv.at[v], rsem.at[v]).wait()
        through, acc = carry[0], carry[1:]
        passing = 1.0 - recv[v, 3 * n : 4 * n, :]
        weight = jnp.where(back, 1.0, through)
        keep = jnp.where(back, passing, 1.0)
        acc = [keep * acc[c] + weight * recv[v, c * n : (c + 1) * n, :] for c in range(3)]
        return (through * passing, *acc)

    zero = jnp.zeros(small, jnp.float32)
    merged = lax.fori_loop(0, views, merge, (jnp.ones(small, jnp.float32), zero, zero, zero))
    pixels = list(merged[1:]) + [1.0 - merged[0]]
    for c in range(4):
        for r in range(n):
            out[c : c + 1, r * LANES : (r + 1) * LANES] = pixels[c][r : r + 1, :]

    def finish(x, carry):
        for j in range(plan.groups):
            send_piece(x, j, False)
        return carry

    lax.fori_loop(0, plan.nx, finish, 0)
    for k in range(1, lights):
        occ_copy(k).wait_send()
        for i in range(plan.cx):
            dens_copy(k, i).wait_send()


def body(density, occupied, view_sign, transfer, absorb, light_in):
    cells_x, cells_y, columns = density.shape
    plan = Plan(
        lax.axis_size("light"), lax.axis_size("view"), cells_x, cells_y, columns, occupied.shape[2]
    )
    lights, views = plan.lights, plan.views
    n = plan.piece_rows
    f32 = jnp.float32
    hbm = pl.BlockSpec(memory_space=pl.ANY)
    dma = pltpu.SemaphoreType.DMA
    return pl.pallas_call(
        functools.partial(kernel, plan),
        out_shape=pltpu.VMEM((4, n * LANES), f32),
        in_specs=[hbm] * 6,
        out_specs=pl.BlockSpec(memory_space=pltpu.VMEM),
        scratch_shapes=[
            pltpu.SMEM((1, 1), f32),
            pltpu.SMEM(transfer.shape, f32),
            pltpu.SMEM(absorb.shape, f32),
            pltpu.VMEM((lights,) + occupied.shape[1:], occupied.dtype),
            pltpu.VMEM((plan.nx + 2, cells_y, plan.width), density.dtype),
            pltpu.VMEM((3, cells_y, plan.width), f32),
            pltpu.VMEM((lights, plan.tiles, LANES), f32),
            pltpu.VMEM((plan.nx, 3, plan.win_tiles, cells_y, LANES), f32),
            pltpu.VMEM((plan.nx, 3, plan.rows, cells_y, LANES), f32),
            pltpu.VMEM((plan.nx, 4, plan.rows * 8, LANES), f32),
            pltpu.VMEM((3, plan.rows * 8, LANES), f32),
            pltpu.VMEM((3, plan.win_tiles, cells_y, LANES), f32),
            pltpu.VMEM((plan.nx, plan.groups, 4 * n, LANES), f32),
            pltpu.VMEM((views, 4 * n, LANES), f32),
            dma((plan.nx,)),
            dma((lights, cells_x)),
            dma((lights,)),
            dma((lights,)),
            dma((5,)),
            dma((plan.nx, plan.groups)),
            dma((views,)),
        ],
        compiler_params=pltpu.CompilerParams(
            collective_id=0, has_side_effects=True, vmem_limit_bytes=62 * 1024 * 1024
        ),
    )(density, occupied, view_sign.reshape(1, 1), transfer, absorb, light_in)


def solution(mesh):
    in_specs = (
        P("light", "view", None),
        P("light", "view", None),
        P(),
        P(),
        P(),
        P(None, "view", None),
    )
    out_specs = P(None, ("light", "view"))
    return jax.shard_map(body, mesh=mesh, in_specs=in_specs, out_specs=out_specs, check_vma=False)
```

```python
import functools

import jax
import jax.numpy as jnp
from jax import lax
from jax.experimental import pallas as pl
from jax.experimental.pallas import tpu as pltpu
from jax.sharding import PartitionSpec as P

LANES = 128
MESH = pl.DeviceIdType.MESH


class Plan:
    def __init__(self, lights, views, cells_x, cells_y, columns, bricks):
        self.lights, self.views = lights, views
        self.cx, self.cy = cells_x, cells_y
        self.nx, self.ny = cells_x * lights, cells_y * views
        self.tiles = columns // LANES
        self.rows = self.tiles // lights
        self.win_tiles = self.rows + (2 if lights > 2 else 1)
        self.width = self.win_tiles * LANES
        self.piece_rows = cells_x * self.tiles // views
        self.groups = self.rows // self.piece_rows
        self.per_layer = self.tiles // self.piece_rows
        self.tiles_per_brick = self.tiles // bricks
        self.bricks = bricks

    def window(self, light):
        return jnp.clip(light * self.rows - 1, 0, self.tiles - self.win_tiles)


def cubic(coeffs, x):
    return coeffs[0] + x * (coeffs[1] + x * (coeffs[2] + x * coeffs[3]))


def kernel(
    plan,
    density,
    occupied_hbm,
    view_sign_hbm,
    transfer_hbm,
    absorb_hbm,
    light_in,
    out,
    view_sign,
    transfer,
    absorb,
    bricks,
    wbuf,
    lbuf,
    occ,
    transmit,
    lit,
    base,
    column,
    front,
    image,
    recv,
    dsem,
    dsend,
    osem,
    osend,
    lsem,
    isend,
    rsem,
):
    lights, views, rows, cy = plan.lights, plan.views, plan.rows, plan.cy
    me_l = lax.axis_index("light")
    me_v = lax.axis_index("view")
    win = plan.window(me_l)
    off = me_l * rows - win
    slab_of_me = ((me_v * plan.piece_rows) % plan.tiles) // rows

    small_copies = [
        pltpu.make_async_copy(src, dst, lsem.at[i])
        for i, (src, dst) in enumerate(
            (
                (view_sign_hbm, view_sign),
                (transfer_hbm, transfer),
                (absorb_hbm, absorb),
            )
        )
    ]
    for copy in small_copies:
        copy.start()

    barrier = pltpu.get_barrier_semaphore()
    for k in range(1, lights):
        pl.semaphore_signal(
            barrier, inc=1, device_id={"light": (me_l + k) % lights, "view": me_v}, device_id_type=MESH
        )

    def greet(v, carry):
        @pl.when(jnp.logical_or(v != me_v, slab_of_me != me_l))
        def _():
            pl.semaphore_signal(
                barrier, inc=1, device_id={"light": slab_of_me, "view": v}, device_id_type=MESH
            )

        return carry

    lax.fori_loop(0, views, greet, 0)

    def columns_of(light):
        return pl.ds(pl.multiple_of(plan.window(light) * LANES, LANES), plan.width)

    for i in range(plan.cx):
        layer = me_l * plan.cx + i
        pltpu.make_async_copy(
            density.at[i, :, columns_of(me_l)], wbuf.at[layer + 1], dsem.at[layer]
        ).start()
    light_copy = pltpu.make_async_copy(light_in.at[:, :, columns_of(me_l)], lbuf, lsem.at[4])
    light_copy.start()

    pltpu.make_async_copy(occupied_hbm.at[0], bricks.at[me_l], osem.at[me_l]).start()

    @pl.when(slab_of_me == me_l)
    def _():
        pl.semaphore_wait(barrier, lights - 1 + views - 1)

    @pl.when(slab_of_me != me_l)
    def _():
        pl.semaphore_wait(barrier, lights - 1 + views)

    def occ_copy(k):
        return pltpu.make_async_remote_copy(
            src_ref=occupied_hbm.at[0],
            dst_ref=bricks.at[me_l],
            send_sem=osend.at[k],
            recv_sem=osem.at[me_l],
            device_id={"light": (me_l + k) % lights, "view": me_v},
            device_id_type=MESH,
        )

    def dens_copy(k, i):
        other = (me_l + k) % lights
        layer = me_l * plan.cx + i
        return pltpu.make_async_remote_copy(
            src_ref=density.at[i, :, columns_of(other)],
            dst_ref=wbuf.at[layer + 1],
            send_sem=dsend.at[k, i],
            recv_sem=dsem.at[layer],
            device_id={"light": other, "view": me_v},
            device_id_type=MESH,
        )

    for k in range(1, lights):
        occ_copy(k).start()
    for i in range(plan.cx):
        for k in range(1, lights):
            dens_copy(k, i).start()

    for copy in small_copies:
        copy.wait()

    tile_shape = (cy, LANES)
    lane = lax.broadcasted_iota(jnp.int32, tile_shape, 1)
    first_lane, last_lane = lane == 0, lane == LANES - 1
    sign = jnp.full(tile_shape, view_sign[0, 0])
    path_rate = (-2.0 / plan.ny) / jnp.abs(sign)
    rates = [absorb[c] * (-1.0 / plan.nx) for c in range(3)]
    ext_coeffs = [transfer[0, k] for k in range(4)]
    colour_coeffs = [[transfer[c, k] * 0.5 for k in range(4)] for c in (1, 2, 3)]
    has_left = jnp.where(me_l > 0, 1.0, 0.0)
    has_right = jnp.where(me_l < lights - 1, 1.0, 0.0)

    to = lax.broadcasted_iota(jnp.int32, (cy, cy), 0)
    of = lax.broadcasted_iota(jnp.int32, (cy, cy), 1)
    after_y = (of == jnp.minimum(to + 1, cy - 1)).astype(jnp.float32)
    before_y = (of == jnp.maximum(to - 1, 0)).astype(jnp.float32)
    slope_y = (after_y - before_y).astype(jnp.bfloat16)
    to = lax.broadcasted_iota(jnp.int32, (cy + 8, 2 * cy), 0)
    of = lax.broadcasted_iota(jnp.int32, (cy + 8, 2 * cy), 1) % cy
    one, none = jnp.ones(to.shape, jnp.float32), jnp.zeros(to.shape, jnp.float32)
    near_first = jnp.where(of < to, one, none)
    near_last = jnp.where(of > to, one, none)
    sign_wide = jnp.full(to.shape, view_sign[0, 0])
    in_front = jnp.where(sign_wide < 0.0, near_last, near_first)
    in_front = jnp.where(to >= cy, one, in_front).astype(jnp.bfloat16)

    blank = jnp.zeros((cy, plan.width), wbuf.dtype)
    wbuf[0] = blank
    wbuf[plan.nx + 1] = blank

    places = [off + t for t in range(rows)]
    if lights == 2:
        places += [jnp.where(me_l == 0, rows, 0)]
        halo_masks = [jnp.where(last_lane, has_left, jnp.where(first_lane, has_right, 1.0))]
    else:
        places += [jnp.minimum(off + rows, plan.win_tiles - 1), jnp.maximum(off - 1, 0)]
        halo_masks = [has_right, has_left]

    def tile_at(ref, lead, t):
        return ref[lead, :, pl.ds(pl.multiple_of(t * LANES, LANES), LANES)].astype(jnp.float32)

    def next_to(left, here, right):
        before = pltpu.roll(jnp.where(last_lane, left, here), 1, 1)
        after = pltpu.roll(jnp.where(first_lane, right, here), LANES - 1, 1)
        return before, after

    def wait_layer(x):
        pltpu.make_async_copy(wbuf.at[x + 1], wbuf.at[x + 1], dsem.at[x]).wait()

    tile_of = lax.broadcasted_iota(jnp.int32, (plan.tiles, plan.bricks), 0)
    brick_of = lax.broadcasted_iota(jnp.int32, (plan.tiles, plan.bricks), 1)
    own_brick = tile_of // plan.tiles_per_brick == brick_of

    def wait_occ(block):
        pltpu.make_async_copy(bricks.at[block], bricks.at[block], osem.at[block]).wait()
        row = jnp.broadcast_to(bricks[block], own_brick.shape).astype(jnp.float32)
        held = jnp.sum(jnp.where(own_brick, row, 0.0), axis=1, keepdims=True)
        occ[block] = jnp.broadcast_to(held, (plan.tiles, LANES))

    def prepare(x):
        block = x // plan.cx
        depths = []
        for t, place in enumerate(places):
            held = occ[block, pl.ds(win + place, 1), :]
            cells = tile_at(wbuf, x + 1, place)
            ext = jnp.log(1.0 + jnp.exp(cubic(ext_coeffs, cells))) * held
            if t < rows:
                depths.append(path_rate * ext)
            for c in range(3):
                through = jnp.exp(rates[c] * ext)
                transmit[x, c, t] = through if t < rows else through * halo_masks[t - rows]
        high = [depth.astype(jnp.bfloat16) for depth in depths]
        low = [
            (depth - h.astype(jnp.float32)).astype(jnp.bfloat16) for depth, h in zip(depths, high)
        ]
        stacked = jnp.concatenate(
            [jnp.concatenate(high, axis=1), jnp.concatenate(low, axis=1)], axis=0
        )
        sums = jnp.dot(in_front, stacked, preferred_element_type=jnp.float32)
        own = wbuf[x + 1, :, pl.ds(pl.multiple_of(off * LANES, LANES), rows * LANES)]
        grad_y = jnp.dot(slope_y, own, preferred_element_type=jnp.float32)
        tiles = [tile_at(wbuf, x + 1, jnp.maximum(off - 1, 0)) * has_left]
        tiles += [tile_at(wbuf, x + 1, off + t) for t in range(rows)]
        tiles += [tile_at(wbuf, x + 1, jnp.minimum(off + rows, plan.win_tiles - 1)) * has_right]
        for t in range(rows):
            part = slice(t * LANES, (t + 1) * LANES)
            seen = jnp.exp(sums[:cy, part]) * (1.0 - jnp.exp(depths[t]))
            d = tiles[t + 1]
            before, after = next_to(tiles[t], d, tiles[t + 2])
            gx = tile_at(wbuf, x + 2, off + t) - tile_at(wbuf, x, off + t)
            gy = grad_y[:, part]
            gz = after - before
            facing = (0.14 * gx + 0.063 * gy + 0.084 * gz) * lax.rsqrt(
                4.0 + gx * gx + gy * gy + gz * gz
            )
            shading = 0.325 + facing
            for c in range(3):
                coloured = seen * (1.0 + jnp.tanh(cubic(colour_coeffs[c], d)))
                lit[x, c, t] = coloured * shading
                base[x, c, t * 8 : (t + 1) * 8, :] = 0.1 * sum(
                    coloured[k : k + 8] for k in range(0, cy, 8)
                )
            base[x, 3, t * 8 : (t + 1) * 8, :] = 1.0 - jnp.exp(sums[cy:, part])

    def shine(x):
        pixels = []
        for c in range(3):
            for t in range(rows):
                share = front[c, t] * lit[x, c, t]
                column[c, t * 8 : (t + 1) * 8, :] = base[x, c, t * 8 : (t + 1) * 8, :] + sum(
                    share[k : k + 8] for k in range(0, cy, 8)
                )
            prods = [front[c, t] * transmit[x, c, t] for t in range(plan.win_tiles)]
            for t in range(plan.win_tiles):
                before, after = next_to(
                    prods[t - 1], prods[t], prods[(t + 1) % plan.win_tiles]
                )
                front[c, t] = 0.5 * prods[t] + 0.25 * (before + after)
        for c in range(3):
            pixels.append(sum(column[c, pl.ds(r, rows, stride=8), :] for r in range(8)))
        pixels.append(base[x, 3, pl.ds(0, rows, stride=8), :])
        n = plan.piece_rows
        for j in range(plan.groups):
            for c in range(4):
                image[x, j, c * n : (c + 1) * n, :] = pixels[c][j * n : (j + 1) * n, :]

    def send_layer(x):
        for j in range(plan.groups):
            send_piece(x, j, True)

    def send_piece(x, j, start):
        owner_l = x // plan.cx
        owner_v = (x % plan.cx) * plan.per_layer + me_l * plan.groups + j
        mine = jnp.logical_and(owner_l == me_l, owner_v == me_v)

        @pl.when(mine)
        def _():
            if start:
                pltpu.make_async_copy(image.at[x, j], recv.at[me_v], rsem.at[me_v]).start()

        @pl.when(jnp.logical_not(mine))
        def _():
            copy = pltpu.make_async_remote_copy(
                src_ref=image.at[x, j],
                dst_ref=recv.at[me_v],
                send_sem=isend.at[x, j],
                recv_sem=rsem.at[me_v],
                device_id={"light": owner_l, "view": owner_v},
                device_id_type=MESH,
            )
            if start:
                copy.start()
            else:
                copy.wait_send()

    start = jnp.where(me_l > 0, me_l * plan.cx + 1, 0)
    lead = jnp.where(me_l > 0, plan.nx - start, 0)

    light_copy.wait()
    for c in range(3):
        for t, place in enumerate(places):
            front[c, t] = tile_at(lbuf, c, place)

    @pl.when(me_l > 0)
    def _():
        wait_layer(start - 1)

    wait_layer(start)
    wait_occ(me_l)

    def arrive(x):
        new = jnp.logical_and(x < plan.nx, jnp.logical_and(x != start, x != start - 1))

        @pl.when(new)
        def _():
            wait_layer(x)

        @pl.when(jnp.logical_and(new, jnp.logical_and(x % plan.cx == 0, x // plan.cx != me_l)))
        def _():
            wait_occ(x // plan.cx)

    def arrive_for(step):
        x = (start + step) % plan.nx

        @pl.when(jnp.logical_and(x == 0, step > 0))
        def _():
            arrive(0)

        arrive(x + 1)
        return x

    def early(step, carry):
        prepare(arrive_for(step))
        return carry

    def both(step, carry):
        x = arrive_for(step)
        shine(x - 1)
        prepare(x)
        send_layer(x - 1)
        return carry

    def late(x, carry):
        shine(x)
        send_layer(x)
        return carry

    lax.fori_loop(0, lead + 1, early, 0)
    lax.fori_loop(lead + 1, plan.nx, both, 0)
    lax.fori_loop(plan.nx - 1 - lead, plan.nx, late, 0)

    n = plan.piece_rows
    small = (n, LANES)
    back = jnp.full(small, view_sign[0, 0]) < 0.0

    def merge(v, carry):
        pltpu.make_async_copy(recv.at[v], recv.at[v], rsem.at[v]).wait()
        through, acc = carry[0], carry[1:]
        passing = 1.0 - recv[v, 3 * n : 4 * n, :]
        weight = jnp.where(back, 1.0, through)
        keep = jnp.where(back, passing, 1.0)
        acc = [keep * acc[c] + weight * recv[v, c * n : (c + 1) * n, :] for c in range(3)]
        return (through * passing, *acc)

    zero = jnp.zeros(small, jnp.float32)
    merged = lax.fori_loop(0, views, merge, (jnp.ones(small, jnp.float32), zero, zero, zero))
    pixels = list(merged[1:]) + [1.0 - merged[0]]
    for c in range(4):
        for r in range(n):
            out[c : c + 1, r * LANES : (r + 1) * LANES] = pixels[c][r : r + 1, :]

    def finish(x, carry):
        for j in range(plan.groups):
            send_piece(x, j, False)
        return carry

    lax.fori_loop(0, plan.nx, finish, 0)
    for k in range(1, lights):
        occ_copy(k).wait_send()
        for i in range(plan.cx):
            dens_copy(k, i).wait_send()


def body(density, occupied, view_sign, transfer, absorb, light_in):
    cells_x, cells_y, columns = density.shape
    plan = Plan(
        lax.axis_size("light"), lax.axis_size("view"), cells_x, cells_y, columns, occupied.shape[2]
    )
    lights, views = plan.lights, plan.views
    n = plan.piece_rows
    f32 = jnp.float32
    hbm = pl.BlockSpec(memory_space=pl.ANY)
    dma = pltpu.SemaphoreType.DMA
    return pl.pallas_call(
        functools.partial(kernel, plan),
        out_shape=pltpu.VMEM((4, n * LANES), f32),
        in_specs=[hbm] * 6,
        out_specs=pl.BlockSpec(memory_space=pltpu.VMEM),
        scratch_shapes=[
            pltpu.SMEM((1, 1), f32),
            pltpu.SMEM(transfer.shape, f32),
            pltpu.SMEM(absorb.shape, f32),
            pltpu.VMEM((lights,) + occupied.shape[1:], occupied.dtype),
            pltpu.VMEM((plan.nx + 2, cells_y, plan.width), density.dtype),
            pltpu.VMEM((3, cells_y, plan.width), f32),
            pltpu.VMEM((lights, plan.tiles, LANES), f32),
            pltpu.VMEM((plan.nx, 3, plan.win_tiles, cells_y, LANES), f32),
            pltpu.VMEM((plan.nx, 3, plan.rows, cells_y, LANES), f32),
            pltpu.VMEM((plan.nx, 4, plan.rows * 8, LANES), f32),
            pltpu.VMEM((3, plan.rows * 8, LANES), f32),
            pltpu.VMEM((3, plan.win_tiles, cells_y, LANES), f32),
            pltpu.VMEM((plan.nx, plan.groups, 4 * n, LANES), f32),
            pltpu.VMEM((views, 4 * n, LANES), f32),
            dma((plan.nx,)),
            dma((lights, cells_x)),
            dma((lights,)),
            dma((lights,)),
            dma((5,)),
            dma((plan.nx, plan.groups)),
            dma((views,)),
        ],
        compiler_params=pltpu.CompilerParams(
            collective_id=0, has_side_effects=True, vmem_limit_bytes=62 * 1024 * 1024
        ),
    )(density, occupied, view_sign.reshape(1, 1), transfer, absorb, light_in)


def solution(mesh):
    in_specs = (
        P("light", "view", None),
        P("light", "view", None),
        P(),
        P(),
        P(),
        P(None, "view", None),
    )
    out_specs = P(None, ("light", "view"))
    return jax.shard_map(body, mesh=mesh, in_specs=in_specs, out_specs=out_specs, check_vma=False)
```

```python
import functools

import jax
import jax.numpy as jnp
from jax import lax
from jax.experimental import pallas as pl
from jax.experimental.pallas import tpu as pltpu
from jax.sharding import PartitionSpec as P

LANES = 128
MESH = pl.DeviceIdType.MESH


class Plan:
    def __init__(self, lights, views, cells_x, cells_y, columns, bricks):
        self.lights, self.views = lights, views
        self.cx, self.cy = cells_x, cells_y
        self.nx, self.ny = cells_x * lights, cells_y * views
        self.tiles = columns // LANES
        self.rows = self.tiles // lights
        self.win_tiles = self.rows + (2 if lights > 2 else 1)
        self.width = self.win_tiles * LANES
        self.piece_rows = cells_x * self.tiles // views
        self.groups = self.rows // self.piece_rows
        self.per_layer = self.tiles // self.piece_rows
        self.tiles_per_brick = self.tiles // bricks
        self.bricks = bricks

    def window(self, light):
        return jnp.clip(light * self.rows - 1, 0, self.tiles - self.win_tiles)


def cubic(coeffs, x):
    return coeffs[0] + x * (coeffs[1] + x * (coeffs[2] + x * coeffs[3]))


def kernel(
    plan,
    density,
    occupied_hbm,
    view_sign_hbm,
    transfer_hbm,
    absorb_hbm,
    light_in,
    out,
    view_sign,
    transfer,
    absorb,
    bricks,
    wbuf,
    lbuf,
    occ,
    transmit,
    lit,
    base,
    column,
    front,
    image,
    recv,
    dsem,
    dsend,
    osem,
    osend,
    lsem,
    isend,
    rsem,
):
    lights, views, rows, cy = plan.lights, plan.views, plan.rows, plan.cy
    me_l = lax.axis_index("light")
    me_v = lax.axis_index("view")
    win = plan.window(me_l)
    off = me_l * rows - win
    slab_of_me = ((me_v * plan.piece_rows) % plan.tiles) // rows

    small_copies = [
        pltpu.make_async_copy(src, dst, lsem.at[i])
        for i, (src, dst) in enumerate(
            (
                (view_sign_hbm, view_sign),
                (transfer_hbm, transfer),
                (absorb_hbm, absorb),
            )
        )
    ]
    for copy in small_copies:
        copy.start()

    barrier = pltpu.get_barrier_semaphore()
    for k in range(1, lights):
        pl.semaphore_signal(
            barrier, inc=1, device_id={"light": (me_l + k) % lights, "view": me_v}, device_id_type=MESH
        )

    def greet(v, carry):
        @pl.when(jnp.logical_or(v != me_v, slab_of_me != me_l))
        def _():
            pl.semaphore_signal(
                barrier, inc=1, device_id={"light": slab_of_me, "view": v}, device_id_type=MESH
            )

        return carry

    lax.fori_loop(0, views, greet, 0)

    def columns_of(light):
        return pl.ds(pl.multiple_of(plan.window(light) * LANES, LANES), plan.width)

    for i in range(plan.cx):
        layer = me_l * plan.cx + i
        pltpu.make_async_copy(
            density.at[i, :, columns_of(me_l)], wbuf.at[layer + 1], dsem.at[layer]
        ).start()
    light_copy = pltpu.make_async_copy(light_in.at[:, :, columns_of(me_l)], lbuf, lsem.at[4])
    light_copy.start()

    pltpu.make_async_copy(occupied_hbm.at[0], bricks.at[me_l], osem.at[me_l]).start()

    @pl.when(slab_of_me == me_l)
    def _():
        pl.semaphore_wait(barrier, lights - 1 + views - 1)

    @pl.when(slab_of_me != me_l)
    def _():
        pl.semaphore_wait(barrier, lights - 1 + views)

    def occ_copy(k):
        return pltpu.make_async_remote_copy(
            src_ref=occupied_hbm.at[0],
            dst_ref=bricks.at[me_l],
            send_sem=osend.at[k],
            recv_sem=osem.at[me_l],
            device_id={"light": (me_l + k) % lights, "view": me_v},
            device_id_type=MESH,
        )

    def dens_copy(k, i):
        other = (me_l + k) % lights
        layer = me_l * plan.cx + i
        return pltpu.make_async_remote_copy(
            src_ref=density.at[i, :, columns_of(other)],
            dst_ref=wbuf.at[layer + 1],
            send_sem=dsend.at[k, i],
            recv_sem=dsem.at[layer],
            device_id={"light": other, "view": me_v},
            device_id_type=MESH,
        )

    for k in range(1, lights):
        occ_copy(k).start()
    for i in range(plan.cx):
        for k in range(1, lights):
            dens_copy(k, i).start()

    for copy in small_copies:
        copy.wait()

    tile_shape = (cy, LANES)
    lane = lax.broadcasted_iota(jnp.int32, tile_shape, 1)
    first_lane, last_lane = lane == 0, lane == LANES - 1
    sign = jnp.full(tile_shape, view_sign[0, 0])
    path_rate = (-2.0 / plan.ny) / jnp.abs(sign)
    rates = [absorb[c] * (-1.0 / plan.nx) for c in range(3)]
    ext_coeffs = [transfer[0, k] for k in range(4)]
    colour_coeffs = [[transfer[c, k] * 0.5 for k in range(4)] for c in (1, 2, 3)]
    has_left = jnp.where(me_l > 0, 1.0, 0.0)
    has_right = jnp.where(me_l < lights - 1, 1.0, 0.0)

    to = lax.broadcasted_iota(jnp.int32, (cy, cy), 0)
    of = lax.broadcasted_iota(jnp.int32, (cy, cy), 1)
    after_y = (of == jnp.minimum(to + 1, cy - 1)).astype(jnp.float32)
    before_y = (of == jnp.maximum(to - 1, 0)).astype(jnp.float32)
    slope_y = (after_y - before_y).astype(jnp.bfloat16)
    to = lax.broadcasted_iota(jnp.int32, (cy + 8, 2 * cy), 0)
    of = lax.broadcasted_iota(jnp.int32, (cy + 8, 2 * cy), 1) % cy
    one, none = jnp.ones(to.shape, jnp.float32), jnp.zeros(to.shape, jnp.float32)
    near_first = jnp.where(of < to, one, none)
    near_last = jnp.where(of > to, one, none)
    sign_wide = jnp.full(to.shape, view_sign[0, 0])
    in_front = jnp.where(sign_wide < 0.0, near_last, near_first)
    in_front = jnp.where(to >= cy, one, in_front).astype(jnp.bfloat16)

    blank = jnp.zeros((cy, plan.width), wbuf.dtype)
    wbuf[0] = blank
    wbuf[plan.nx + 1] = blank

    places = [off + t for t in range(rows)]
    if lights == 2:
        places += [jnp.where(me_l == 0, rows, 0)]
        halo_masks = [jnp.where(last_lane, has_left, jnp.where(first_lane, has_right, 1.0))]
    else:
        places += [jnp.minimum(off + rows, plan.win_tiles - 1), jnp.maximum(off - 1, 0)]
        halo_masks = [has_right, has_left]

    def tile_at(ref, lead, t):
        return ref[lead, :, pl.ds(pl.multiple_of(t * LANES, LANES), LANES)].astype(jnp.float32)

    def next_to(left, here, right):
        before = pltpu.roll(jnp.where(last_lane, left, here), 1, 1)
        after = pltpu.roll(jnp.where(first_lane, right, here), LANES - 1, 1)
        return before, after

    def wait_layer(x):
        pltpu.make_async_copy(wbuf.at[x + 1], wbuf.at[x + 1], dsem.at[x]).wait()

    tile_of = lax.broadcasted_iota(jnp.int32, (plan.tiles, plan.bricks), 0)
    brick_of = lax.broadcasted_iota(jnp.int32, (plan.tiles, plan.bricks), 1)
    own_brick = tile_of // plan.tiles_per_brick == brick_of

    def wait_occ(block):
        pltpu.make_async_copy(bricks.at[block], bricks.at[block], osem.at[block]).wait()
        row = jnp.broadcast_to(bricks[block], own_brick.shape).astype(jnp.float32)
        held = jnp.sum(jnp.where(own_brick, row, 0.0), axis=1, keepdims=True)
        occ[block] = jnp.broadcast_to(held, (plan.tiles, LANES))

    def prepare(x):
        block = x // plan.cx
        depths = []
        for t, place in enumerate(places):
            held = occ[block, pl.ds(win + place, 1), :]
            cells = tile_at(wbuf, x + 1, place)
            ext = jnp.log(1.0 + jnp.exp(cubic(ext_coeffs, cells))) * held
            if t < rows:
                depths.append(path_rate * ext)
            for c in range(3):
                through = jnp.exp(rates[c] * ext)
                transmit[x, c, t] = through if t < rows else through * halo_masks[t - rows]
        high = [depth.astype(jnp.bfloat16) for depth in depths]
        low = [
            (depth - h.astype(jnp.float32)).astype(jnp.bfloat16) for depth, h in zip(depths, high)
        ]
        stacked = jnp.concatenate(
            [jnp.concatenate(high, axis=1), jnp.concatenate(low, axis=1)], axis=0
        )
        sums = jnp.dot(in_front, stacked, preferred_element_type=jnp.float32)
        own = wbuf[x + 1, :, pl.ds(pl.multiple_of(off * LANES, LANES), rows * LANES)]
        grad_y = jnp.dot(slope_y, own, preferred_element_type=jnp.float32)
        tiles = [tile_at(wbuf, x + 1, jnp.maximum(off - 1, 0)) * has_left]
        tiles += [tile_at(wbuf, x + 1, off + t) for t in range(rows)]
        tiles += [tile_at(wbuf, x + 1, jnp.minimum(off + rows, plan.win_tiles - 1)) * has_right]
        for t in range(rows):
            part = slice(t * LANES, (t + 1) * LANES)
            seen = jnp.exp(sums[:cy, part]) * (1.0 - jnp.exp(depths[t]))
            d = tiles[t + 1]
            before, after = next_to(tiles[t], d, tiles[t + 2])
            gx = tile_at(wbuf, x + 2, off + t) - tile_at(wbuf, x, off + t)
            gy = grad_y[:, part]
            gz = after - before
            facing = (0.14 * gx + 0.063 * gy + 0.084 * gz) * lax.rsqrt(
                4.0 + gx * gx + gy * gy + gz * gz
            )
            shading = 0.325 + facing
            for c in range(3):
                coloured = seen * (1.0 + jnp.tanh(cubic(colour_coeffs[c], d)))
                lit[x, c, t] = coloured * shading
                base[x, c, t * 8 : (t + 1) * 8, :] = 0.1 * sum(
                    coloured[k : k + 8] for k in range(0, cy, 8)
                )
            base[x, 3, t * 8 : (t + 1) * 8, :] = 1.0 - jnp.exp(sums[cy:, part])

    def shine(x):
        pixels = []
        for c in range(3):
            for t in range(rows):
                share = front[c, t] * lit[x, c, t]
                column[c, t * 8 : (t + 1) * 8, :] = base[x, c, t * 8 : (t + 1) * 8, :] + sum(
                    share[k : k + 8] for k in range(0, cy, 8)
                )
            prods = [front[c, t] * transmit[x, c, t] for t in range(plan.win_tiles)]
            for t in range(plan.win_tiles):
                before, after = next_to(
                    prods[t - 1], prods[t], prods[(t + 1) % plan.win_tiles]
                )
                front[c, t] = 0.5 * prods[t] + 0.25 * (before + after)
        for c in range(3):
            pixels.append(sum(column[c, pl.ds(r, rows, stride=8), :] for r in range(8)))
        pixels.append(base[x, 3, pl.ds(0, rows, stride=8), :])
        n = plan.piece_rows
        for j in range(plan.groups):
            for c in range(4):
                image[x, j, c * n : (c + 1) * n, :] = pixels[c][j * n : (j + 1) * n, :]

    def send_layer(x):
        for j in range(plan.groups):
            send_piece(x, j, True)

    def send_piece(x, j, start):
        owner_l = x // plan.cx
        owner_v = (x % plan.cx) * plan.per_layer + me_l * plan.groups + j
        mine = jnp.logical_and(owner_l == me_l, owner_v == me_v)

        @pl.when(mine)
        def _():
            if start:
                pltpu.make_async_copy(image.at[x, j], recv.at[me_v], rsem.at[me_v]).start()

        @pl.when(jnp.logical_not(mine))
        def _():
            copy = pltpu.make_async_remote_copy(
                src_ref=image.at[x, j],
                dst_ref=recv.at[me_v],
                send_sem=isend.at[x, j],
                recv_sem=rsem.at[me_v],
                device_id={"light": owner_l, "view": owner_v},
                device_id_type=MESH,
            )
            if start:
                copy.start()
            else:
                copy.wait_send()

    start = jnp.where(me_l > 0, me_l * plan.cx + 1, 0)
    lead = jnp.where(me_l > 0, plan.nx - start, 0)

    light_copy.wait()
    for c in range(3):
        for t, place in enumerate(places):
            front[c, t] = tile_at(lbuf, c, place)

    @pl.when(me_l > 0)
    def _():
        wait_layer(start - 1)

    wait_layer(start)
    wait_occ(me_l)

    def arrive(x):
        new = jnp.logical_and(x < plan.nx, jnp.logical_and(x != start, x != start - 1))

        @pl.when(new)
        def _():
            wait_layer(x)

        @pl.when(jnp.logical_and(new, jnp.logical_and(x % plan.cx == 0, x // plan.cx != me_l)))
        def _():
            wait_occ(x // plan.cx)

    def early(step, carry):
        x = start + step
        arrive(x + 1)
        prepare(x)
        return carry

    def both(step, carry):
        x = (start + step) % plan.nx

        @pl.when(jnp.logical_and(x == 0, step > 0))
        def _():
            arrive(0)

        arrive(x + 1)
        prepare(x)
        shine(x)
        send_layer(x)
        return carry

    def late(x, carry):
        shine(x)
        send_layer(x)
        return carry

    lax.fori_loop(0, lead, early, 0)
    lax.fori_loop(lead, plan.nx, both, 0)
    lax.fori_loop(plan.nx - lead, plan.nx, late, 0)

    def finish(x, carry):
        for j in range(plan.groups):
            send_piece(x, j, False)
        return carry

    for k in range(1, lights):
        occ_copy(k).wait_send()
        for i in range(plan.cx):
            dens_copy(k, i).wait_send()
    lax.fori_loop(0, plan.nx, finish, 0)

    n = plan.piece_rows
    small = (n, LANES)
    back = jnp.full(small, view_sign[0, 0]) < 0.0

    def wait_piece(v, carry):
        pltpu.make_async_copy(recv.at[v], recv.at[v], rsem.at[v]).wait()
        return carry

    lax.fori_loop(0, views, wait_piece, 0)
    through = jnp.ones(small, jnp.float32)
    acc = [jnp.zeros(small, jnp.float32) for _ in range(3)]
    for v in range(views):
        passing = 1.0 - recv[v, 3 * n : 4 * n, :]
        weight = jnp.where(back, 1.0, through)
        keep = jnp.where(back, passing, 1.0)
        through = through * passing
        for c in range(3):
            acc[c] = keep * acc[c] + weight * recv[v, c * n : (c + 1) * n, :]
    pixels = acc + [1.0 - through]
    for c in range(4):
        for r in range(n):
            out[c : c + 1, r * LANES : (r + 1) * LANES] = pixels[c][r : r + 1, :]


def body(density, occupied, view_sign, transfer, absorb, light_in):
    cells_x, cells_y, columns = density.shape
    plan = Plan(
        lax.axis_size("light"), lax.axis_size("view"), cells_x, cells_y, columns, occupied.shape[2]
    )
    lights, views = plan.lights, plan.views
    n = plan.piece_rows
    f32 = jnp.float32
    hbm = pl.BlockSpec(memory_space=pl.ANY)
    dma = pltpu.SemaphoreType.DMA
    return pl.pallas_call(
        functools.partial(kernel, plan),
        out_shape=pltpu.VMEM((4, n * LANES), f32),
        in_specs=[hbm] * 6,
        out_specs=pl.BlockSpec(memory_space=pltpu.VMEM),
        scratch_shapes=[
            pltpu.SMEM((1, 1), f32),
            pltpu.SMEM(transfer.shape, f32),
            pltpu.SMEM(absorb.shape, f32),
            pltpu.VMEM((lights,) + occupied.shape[1:], occupied.dtype),
            pltpu.VMEM((plan.nx + 2, cells_y, plan.width), density.dtype),
            pltpu.VMEM((3, cells_y, plan.width), f32),
            pltpu.VMEM((lights, plan.tiles, LANES), f32),
            pltpu.VMEM((plan.nx, 3, plan.win_tiles, cells_y, LANES), f32),
            pltpu.VMEM((plan.nx, 3, plan.rows, cells_y, LANES), f32),
            pltpu.VMEM((plan.nx, 4, plan.rows * 8, LANES), f32),
            pltpu.VMEM((3, plan.rows * 8, LANES), f32),
            pltpu.VMEM((3, plan.win_tiles, cells_y, LANES), f32),
            pltpu.VMEM((plan.nx, plan.groups, 4 * n, LANES), f32),
            pltpu.VMEM((views, 4 * n, LANES), f32),
            dma((plan.nx,)),
            dma((lights, cells_x)),
            dma((lights,)),
            dma((lights,)),
            dma((5,)),
            dma((plan.nx, plan.groups)),
            dma((views,)),
        ],
        compiler_params=pltpu.CompilerParams(
            collective_id=0, has_side_effects=True, vmem_limit_bytes=62 * 1024 * 1024
        ),
    )(density, occupied, view_sign.reshape(1, 1), transfer, absorb, light_in)


def solution(mesh):
    in_specs = (
        P("light", "view", None),
        P("light", "view", None),
        P(),
        P(),
        P(),
        P(None, "view", None),
    )
    out_specs = P(None, ("light", "view"))
    return jax.shard_map(body, mesh=mesh, in_specs=in_specs, out_specs=out_specs, check_vma=False)
```

```python
import functools

import jax
import jax.numpy as jnp
from jax import lax
from jax.experimental import pallas as pl
from jax.experimental.pallas import tpu as pltpu
from jax.sharding import PartitionSpec as P

LANES = 128
MESH = pl.DeviceIdType.MESH


class Plan:
    def __init__(self, lights, views, cells_x, cells_y, columns, bricks):
        self.lights, self.views = lights, views
        self.cx, self.cy = cells_x, cells_y
        self.nx, self.ny = cells_x * lights, cells_y * views
        self.tiles = columns // LANES
        self.rows = self.tiles // lights
        self.win_tiles = self.rows + (2 if lights > 2 else 1)
        self.width = self.win_tiles * LANES
        self.piece_rows = cells_x * self.tiles // views
        self.groups = self.rows // self.piece_rows
        self.per_layer = self.tiles // self.piece_rows
        self.tiles_per_brick = self.tiles // bricks
        self.bricks = bricks

    def window(self, light):
        return jnp.clip(light * self.rows - 1, 0, self.tiles - self.win_tiles)


def cubic(coeffs, x):
    return coeffs[0] + x * (coeffs[1] + x * (coeffs[2] + x * coeffs[3]))


def kernel(
    plan,
    density,
    occupied_hbm,
    view_sign_hbm,
    transfer_hbm,
    absorb_hbm,
    light_in,
    out,
    view_sign,
    transfer,
    absorb,
    bricks,
    wbuf,
    lbuf,
    occ,
    transmit,
    lit,
    base,
    column,
    front,
    image,
    recv,
    dsem,
    dsend,
    osem,
    osend,
    lsem,
    isend,
    rsem,
):
    lights, views, rows, cy = plan.lights, plan.views, plan.rows, plan.cy
    me_l = lax.axis_index("light")
    me_v = lax.axis_index("view")
    win = plan.window(me_l)
    off = me_l * rows - win
    slab_of_me = ((me_v * plan.piece_rows) % plan.tiles) // rows

    small_copies = [
        pltpu.make_async_copy(src, dst, lsem.at[i])
        for i, (src, dst) in enumerate(
            (
                (view_sign_hbm, view_sign),
                (transfer_hbm, transfer),
                (absorb_hbm, absorb),
            )
        )
    ]
    for copy in small_copies:
        copy.start()

    barrier = pltpu.get_barrier_semaphore()
    for k in range(1, lights):
        pl.semaphore_signal(
            barrier, inc=1, device_id={"light": (me_l + k) % lights, "view": me_v}, device_id_type=MESH
        )

    def greet(v, carry):
        @pl.when(jnp.logical_or(v != me_v, slab_of_me != me_l))
        def _():
            pl.semaphore_signal(
                barrier, inc=1, device_id={"light": slab_of_me, "view": v}, device_id_type=MESH
            )

        return carry

    lax.fori_loop(0, views, greet, 0)

    def columns_of(light):
        return pl.ds(pl.multiple_of(plan.window(light) * LANES, LANES), plan.width)

    for i in range(plan.cx):
        layer = me_l * plan.cx + i
        pltpu.make_async_copy(
            density.at[i, :, columns_of(me_l)], wbuf.at[layer + 1], dsem.at[layer]
        ).start()
    light_copy = pltpu.make_async_copy(light_in.at[:, :, columns_of(me_l)], lbuf, lsem.at[4])

    pltpu.make_async_copy(occupied_hbm.at[0], bricks.at[me_l], osem.at[me_l]).start()

    @pl.when(slab_of_me == me_l)
    def _():
        pl.semaphore_wait(barrier, lights - 1 + views - 1)

    @pl.when(slab_of_me != me_l)
    def _():
        pl.semaphore_wait(barrier, lights - 1 + views)

    def occ_copy(k):
        return pltpu.make_async_remote_copy(
            src_ref=occupied_hbm.at[0],
            dst_ref=bricks.at[me_l],
            send_sem=osend.at[k],
            recv_sem=osem.at[me_l],
            device_id={"light": (me_l + k) % lights, "view": me_v},
            device_id_type=MESH,
        )

    def dens_copy(k, i):
        other = (me_l + k) % lights
        layer = me_l * plan.cx + i
        return pltpu.make_async_remote_copy(
            src_ref=density.at[i, :, columns_of(other)],
            dst_ref=wbuf.at[layer + 1],
            send_sem=dsend.at[k, i],
            recv_sem=dsem.at[layer],
            device_id={"light": other, "view": me_v},
            device_id_type=MESH,
        )

    for k in range(1, lights):
        occ_copy(k).start()
    for i in range(plan.cx):
        for k in range(1, lights):
            dens_copy(k, i).start()
    light_copy.start()

    for copy in small_copies:
        copy.wait()

    tile_shape = (cy, LANES)
    lane = lax.broadcasted_iota(jnp.int32, tile_shape, 1)
    first_lane, last_lane = lane == 0, lane == LANES - 1
    sign = jnp.full(tile_shape, view_sign[0, 0])
    path_rate = (-2.0 / plan.ny) / jnp.abs(sign)
    rates = [absorb[c] * (-1.0 / plan.nx) for c in range(3)]
    ext_coeffs = [transfer[0, k] for k in range(4)]
    colour_coeffs = [[transfer[c, k] * 0.5 for k in range(4)] for c in (1, 2, 3)]
    has_left = jnp.where(me_l > 0, 1.0, 0.0)
    has_right = jnp.where(me_l < lights - 1, 1.0, 0.0)

    to = lax.broadcasted_iota(jnp.int32, (cy, cy), 0)
    of = lax.broadcasted_iota(jnp.int32, (cy, cy), 1)
    after_y = (of == jnp.minimum(to + 1, cy - 1)).astype(jnp.float32)
    before_y = (of == jnp.maximum(to - 1, 0)).astype(jnp.float32)
    slope_y = (after_y - before_y).astype(jnp.bfloat16)
    to = lax.broadcasted_iota(jnp.int32, (cy + 8, 2 * cy), 0)
    of = lax.broadcasted_iota(jnp.int32, (cy + 8, 2 * cy), 1) % cy
    one, none = jnp.ones(to.shape, jnp.float32), jnp.zeros(to.shape, jnp.float32)
    near_first = jnp.where(of < to, one, none)
    near_last = jnp.where(of > to, one, none)
    sign_wide = jnp.full(to.shape, view_sign[0, 0])
    in_front = jnp.where(sign_wide < 0.0, near_last, near_first)
    in_front = jnp.where(to >= cy, one, in_front).astype(jnp.bfloat16)

    blank = jnp.zeros((cy, plan.width), wbuf.dtype)
    wbuf[0] = blank
    wbuf[plan.nx + 1] = blank

    places = [off + t for t in range(rows)]
    if lights == 2:
        places += [jnp.where(me_l == 0, rows, 0)]
        halo_masks = [jnp.where(last_lane, has_left, jnp.where(first_lane, has_right, 1.0))]
    else:
        places += [jnp.minimum(off + rows, plan.win_tiles - 1), jnp.maximum(off - 1, 0)]
        halo_masks = [has_right, has_left]

    def tile_at(ref, lead, t):
        return ref[lead, :, pl.ds(pl.multiple_of(t * LANES, LANES), LANES)].astype(jnp.float32)

    def next_to(left, here, right):
        before = pltpu.roll(jnp.where(last_lane, left, here), 1, 1)
        after = pltpu.roll(jnp.where(first_lane, right, here), LANES - 1, 1)
        return before, after

    def wait_layer(x):
        pltpu.make_async_copy(wbuf.at[x + 1], wbuf.at[x + 1], dsem.at[x]).wait()

    tile_of = lax.broadcasted_iota(jnp.int32, (plan.tiles, plan.bricks), 0)
    brick_of = lax.broadcasted_iota(jnp.int32, (plan.tiles, plan.bricks), 1)
    own_brick = tile_of // plan.tiles_per_brick == brick_of

    def wait_occ(block):
        pltpu.make_async_copy(bricks.at[block], bricks.at[block], osem.at[block]).wait()
        row = jnp.broadcast_to(bricks[block], own_brick.shape).astype(jnp.float32)
        held = jnp.sum(jnp.where(own_brick, row, 0.0), axis=1, keepdims=True)
        occ[block] = jnp.broadcast_to(held, (plan.tiles, LANES))

    def prepare(x):
        block = x // plan.cx
        depths = []
        for t, place in enumerate(places):
            held = occ[block, pl.ds(win + place, 1), :]
            cells = tile_at(wbuf, x + 1, place)
            ext = jnp.log(1.0 + jnp.exp(cubic(ext_coeffs, cells))) * held
            if t < rows:
                depths.append(path_rate * ext)
            for c in range(3):
                through = jnp.exp(rates[c] * ext)
                transmit[x, c, t] = through if t < rows else through * halo_masks[t - rows]
        high = [depth.astype(jnp.bfloat16) for depth in depths]
        low = [
            (depth - h.astype(jnp.float32)).astype(jnp.bfloat16) for depth, h in zip(depths, high)
        ]
        stacked = jnp.concatenate(
            [jnp.concatenate(high, axis=1), jnp.concatenate(low, axis=1)], axis=0
        )
        sums = jnp.dot(in_front, stacked, preferred_element_type=jnp.float32)
        own = wbuf[x + 1, :, pl.ds(pl.multiple_of(off * LANES, LANES), rows * LANES)]
        grad_y = jnp.dot(slope_y, own, preferred_element_type=jnp.float32)
        tiles = [tile_at(wbuf, x + 1, jnp.maximum(off - 1, 0)) * has_left]
        tiles += [tile_at(wbuf, x + 1, off + t) for t in range(rows)]
        tiles += [tile_at(wbuf, x + 1, jnp.minimum(off + rows, plan.win_tiles - 1)) * has_right]
        for t in range(rows):
            part = slice(t * LANES, (t + 1) * LANES)
            seen = jnp.exp(sums[:cy, part]) * (1.0 - jnp.exp(depths[t]))
            d = tiles[t + 1]
            before, after = next_to(tiles[t], d, tiles[t + 2])
            gx = tile_at(wbuf, x + 2, off + t) - tile_at(wbuf, x, off + t)
            gy = grad_y[:, part]
            gz = after - before
            facing = (0.14 * gx + 0.063 * gy + 0.084 * gz) * lax.rsqrt(
                4.0 + gx * gx + gy * gy + gz * gz
            )
            shading = 0.325 + facing
            for c in range(3):
                coloured = seen * (1.0 + jnp.tanh(cubic(colour_coeffs[c], d)))
                lit[x, c, t] = coloured * shading
                base[x, c, t * 8 : (t + 1) * 8, :] = 0.1 * sum(
                    coloured[k : k + 8] for k in range(0, cy, 8)
                )
            base[x, 3, t * 8 : (t + 1) * 8, :] = 1.0 - jnp.exp(sums[cy:, part])

    def shine(x):
        pixels = []
        for c in range(3):
            for t in range(rows):
                share = front[c, t] * lit[x, c, t]
                column[c, t * 8 : (t + 1) * 8, :] = base[x, c, t * 8 : (t + 1) * 8, :] + sum(
                    share[k : k + 8] for k in range(0, cy, 8)
                )
            prods = [front[c, t] * transmit[x, c, t] for t in range(plan.win_tiles)]
            for t in range(plan.win_tiles):
                before, after = next_to(
                    prods[t - 1], prods[t], prods[(t + 1) % plan.win_tiles]
                )
                front[c, t] = 0.5 * prods[t] + 0.25 * (before + after)
        for c in range(3):
            pixels.append(sum(column[c, pl.ds(r, rows, stride=8), :] for r in range(8)))
        pixels.append(base[x, 3, pl.ds(0, rows, stride=8), :])
        n = plan.piece_rows
        for j in range(plan.groups):
            for c in range(4):
                image[x, j, c * n : (c + 1) * n, :] = pixels[c][j * n : (j + 1) * n, :]

    def send_layer(x):
        for j in range(plan.groups):
            send_piece(x, j, True)

    def send_piece(x, j, start):
        owner_l = x // plan.cx
        owner_v = (x % plan.cx) * plan.per_layer + me_l * plan.groups + j
        mine = jnp.logical_and(owner_l == me_l, owner_v == me_v)

        @pl.when(mine)
        def _():
            if start:
                pltpu.make_async_copy(image.at[x, j], recv.at[me_v], rsem.at[me_v]).start()

        @pl.when(jnp.logical_not(mine))
        def _():
            copy = pltpu.make_async_remote_copy(
                src_ref=image.at[x, j],
                dst_ref=recv.at[me_v],
                send_sem=isend.at[x, j],
                recv_sem=rsem.at[me_v],
                device_id={"light": owner_l, "view": owner_v},
                device_id_type=MESH,
            )
            if start:
                copy.start()
            else:
                copy.wait_send()

    start = jnp.where(me_l > 0, me_l * plan.cx + 1, 0)
    lead = jnp.where(me_l > 0, plan.nx - start, 0)

    @pl.when(me_l > 0)
    def _():
        wait_layer(start - 1)

    wait_layer(start)
    wait_occ(me_l)

    def arrive(x):
        new = jnp.logical_and(x < plan.nx, jnp.logical_and(x != start, x != start - 1))

        @pl.when(new)
        def _():
            wait_layer(x)

        @pl.when(jnp.logical_and(new, jnp.logical_and(x % plan.cx == 0, x // plan.cx != me_l)))
        def _():
            wait_occ(x // plan.cx)

    def early(step, carry):
        x = start + step
        arrive(x + 1)
        prepare(x)
        return carry

    def both(step, carry):
        x = (start + step) % plan.nx

        @pl.when(jnp.logical_and(x == 0, step > 0))
        def _():
            arrive(0)

        arrive(x + 1)
        prepare(x)
        shine(x)
        send_layer(x)
        return carry

    def late(x, carry):
        shine(x)
        send_layer(x)
        return carry

    lax.fori_loop(0, lead, early, 0)

    light_copy.wait()
    for c in range(3):
        for t, place in enumerate(places):
            front[c, t] = tile_at(lbuf, c, place)

    lax.fori_loop(lead, plan.nx, both, 0)
    lax.fori_loop(plan.nx - lead, plan.nx, late, 0)

    n = plan.piece_rows
    small = (n, LANES)
    back = jnp.full(small, view_sign[0, 0]) < 0.0

    def merge(v, carry):
        pltpu.make_async_copy(recv.at[v], recv.at[v], rsem.at[v]).wait()
        through, acc = carry[0], carry[1:]
        passing = 1.0 - recv[v, 3 * n : 4 * n, :]
        weight = jnp.where(back, 1.0, through)
        keep = jnp.where(back, passing, 1.0)
        acc = [keep * acc[c] + weight * recv[v, c * n : (c + 1) * n, :] for c in range(3)]
        return (through * passing, *acc)

    zero = jnp.zeros(small, jnp.float32)
    merged = lax.fori_loop(0, views, merge, (jnp.ones(small, jnp.float32), zero, zero, zero))
    pixels = list(merged[1:]) + [1.0 - merged[0]]
    for c in range(4):
        for r in range(n):
            out[c : c + 1, r * LANES : (r + 1) * LANES] = pixels[c][r : r + 1, :]

    def finish(x, carry):
        for j in range(plan.groups):
            send_piece(x, j, False)
        return carry

    lax.fori_loop(0, plan.nx, finish, 0)
    for k in range(1, lights):
        occ_copy(k).wait_send()
        for i in range(plan.cx):
            dens_copy(k, i).wait_send()


def body(density, occupied, view_sign, transfer, absorb, light_in):
    cells_x, cells_y, columns = density.shape
    plan = Plan(
        lax.axis_size("light"), lax.axis_size("view"), cells_x, cells_y, columns, occupied.shape[2]
    )
    lights, views = plan.lights, plan.views
    n = plan.piece_rows
    f32 = jnp.float32
    hbm = pl.BlockSpec(memory_space=pl.ANY)
    dma = pltpu.SemaphoreType.DMA
    return pl.pallas_call(
        functools.partial(kernel, plan),
        out_shape=pltpu.VMEM((4, n * LANES), f32),
        in_specs=[hbm] * 6,
        out_specs=pl.BlockSpec(memory_space=pltpu.VMEM),
        scratch_shapes=[
            pltpu.SMEM((1, 1), f32),
            pltpu.SMEM(transfer.shape, f32),
            pltpu.SMEM(absorb.shape, f32),
            pltpu.VMEM((lights,) + occupied.shape[1:], occupied.dtype),
            pltpu.VMEM((plan.nx + 2, cells_y, plan.width), density.dtype),
            pltpu.VMEM((3, cells_y, plan.width), f32),
            pltpu.VMEM((lights, plan.tiles, LANES), f32),
            pltpu.VMEM((plan.nx, 3, plan.win_tiles, cells_y, LANES), f32),
            pltpu.VMEM((plan.nx, 3, plan.rows, cells_y, LANES), f32),
            pltpu.VMEM((plan.nx, 4, plan.rows * 8, LANES), f32),
            pltpu.VMEM((3, plan.rows * 8, LANES), f32),
            pltpu.VMEM((3, plan.win_tiles, cells_y, LANES), f32),
            pltpu.VMEM((plan.nx, plan.groups, 4 * n, LANES), f32),
            pltpu.VMEM((views, 4 * n, LANES), f32),
            dma((plan.nx,)),
            dma((lights, cells_x)),
            dma((lights,)),
            dma((lights,)),
            dma((5,)),
            dma((plan.nx, plan.groups)),
            dma((views,)),
        ],
        compiler_params=pltpu.CompilerParams(
            collective_id=0, has_side_effects=True, vmem_limit_bytes=62 * 1024 * 1024
        ),
    )(density, occupied, view_sign.reshape(1, 1), transfer, absorb, light_in)


def solution(mesh):
    in_specs = (
        P("light", "view", None),
        P("light", "view", None),
        P(),
        P(),
        P(),
        P(None, "view", None),
    )
    out_specs = P(None, ("light", "view"))
    return jax.shard_map(body, mesh=mesh, in_specs=in_specs, out_specs=out_specs, check_vma=False)
```
